256 devices in a mesh: ctx: 16 (over y_lo, z), seq: 16 (over y_hi, x, core).
Axes of the slice: x: 4, y: 4 (y_hi: 2, y_lo: 2; y = y_hi * 2 + y_lo), z: 8, core: 2. Of those that a mesh axis runs over, the one named last changes fastest.
Arguments:
- queries: bfloat16 [65536, 1024], P(('seq', 'ctx')), parts along dimension 0, may hold values from -40 to 40
- keys: bfloat16 [65536, 128], P(('seq', 'ctx')), parts along dimension 0, may hold values from -40 to 40
- values: bfloat16 [65536, 128], P(('seq', 'ctx')), parts along dimension 0, may hold values from -6 to 6
- attn_out: bfloat16 [65536, 1024], P(('seq', 'ctx')), parts along dimension 0, may hold values from -4 to 4
- out_grad: bfloat16 [65536, 1024], P(('seq', 'ctx')), parts along dimension 0, may hold values from -6 to 6
- tile_doc: int32 [512], P('seq'), parts along dimension 0, may hold values from 0 to 7, never falling along the last dimension, each value on 1 to 24 neighbouring positions
Outputs:
- query_grad: bfloat16 [65536, 1024], P(('seq', 'ctx')), parts along dimension 0
- key_grad: bfloat16 [65536, 128], P(('seq', 'ctx')), parts along dimension 0
- value_grad: bfloat16 [65536, 128], P(('seq', 'ctx')), parts along dimension 0
The draws below stay inside these ranges and needn't reach their ends.
There are 16 independent parts, one for each index of `seq`. The reference program is written for one: setup_inputs(seed, part) draws one part's arguments, and reference() takes and returns one part's arrays. A program takes and returns all parts, laid end to end along the dimension named above; each array names one. Nothing has to cross between parts.
Inputs may be any that keep to these rules, and one draw needn't show every extreme that they name: tile_doc never falls; every document covers 1 to 24 consecutive tiles and one covers exactly 24.
All inputs are finite; a program needn't handle non-finite values.
Results may differ from the reference program's by a relative error of at most 0.005.
Values may be sent and summed in bfloat16 or wider, within the bound.
A program may use at most 128 MiB of HBM per device.

```python
import math
import jax
import jax.numpy as jnp
import numpy as np
from jax import lax

HEAD = 128
HEADS = 8
TILE = 128
TOKENS = 4096
TILES = 32
DOCS = 8
MOST_TILES = 24


def draw_queries(key, part):
    key = jax.random.fold_in(key, 11)
    base = jnp.clip(jax.random.normal(key, (TOKENS, HEADS * HEAD), jnp.float32), -6.0, 6.0)
    return base.astype(jnp.bfloat16)


def draw_keys(key, part):
    key = jax.random.fold_in(key, 23)
    base = jnp.clip(jax.random.normal(key, (TOKENS, HEAD), jnp.float32), -6.0, 6.0)
    return base.astype(jnp.bfloat16)


def steps_of(rng, dims, pieces, low, largest):
    def one(dim, parts):
        steps = jax.random.uniform(jax.random.fold_in(jax.random.fold_in(rng, 6), dim), (parts,), jnp.float32, low / len(pieces), largest / len(pieces))
        return jnp.repeat(jnp.exp(steps), dims[dim] // parts).reshape((-1,) + (1,) * (len(dims) - dim - 1))

    factor_of = one(*pieces[0])
    for cut in pieces[1:]:
        factor_of = factor_of * one(*cut)
    return factor_of


def length_profile(amount, total, bound, skew):
    portions = [(1 << 20) // math.isqrt(rank ** skew) + 1 for rank in range(2, amount + 1)]
    spare, holding = total - bound - (amount - 1), [1] * (amount - 1)
    while spare > 0:
        candidates = [i for i in range(amount - 1) if holding[i] < bound]
        mass, left = sum([portions[i] for i in candidates]), spare
        for i in candidates:
            more = min(bound - holding[i], max(1, left * portions[i] // mass), spare)
            holding[i] = holding[i] + more
            spare = spare - more
    return np.array([bound] + holding)


def ragged_sizes(own_key, count, total, bound, lean):
    if count == 2:
        one = jax.random.randint(own_key, (), max(1, total - bound), min(bound, total - 1) + 1)
        return jnp.stack([one, total - one])
    lengths = jnp.asarray(length_profile(count, total, bound, lean), jnp.int32)
    pairs = (count - 1) // 2
    giver, receiver = lengths[1:1 + 2 * pairs:2], lengths[2:2 + 2 * pairs:2]
    room = jnp.minimum(giver - 1, bound - receiver)
    passed = jax.random.randint(jax.random.fold_in(own_key, 1), (pairs,), 0, 1 << 20) % (room + 1)
    lengths = lengths.at[1:1 + 2 * pairs:2].set(giver - passed).at[2:2 + 2 * pairs:2].set(receiver + passed)
    return lengths[jax.random.permutation(jax.random.fold_in(own_key, 2), count)]


def bell_draw(key, shape, spread, most, shards=(), kind=jnp.bfloat16):
    drawn = jax.random.normal(key, shape, jnp.float32) * spread
    if len(shards) > 0:
        drawn = steps_of(key, shape, shards, -0.22, 0.18) * drawn
    return jnp.clip(drawn, min=-most, max=most).astype(kind)


def setup_inputs(seed: int = 0, part: int = 0) -> dict:
    key_list = jax.random.split(jax.random.key(seed), 7)
    part_keys = jax.random.split(jax.random.fold_in(key_list[6], part), 7)
    queries = draw_queries(jax.random.fold_in(jax.random.fold_in(key_list[6], part), 71), part)
    keys = draw_keys(jax.random.fold_in(jax.random.fold_in(key_list[6], part), 71), part)
    values = bell_draw(part_keys[2], (TOKENS, HEAD), 1.0, 6.0, ((0, 16),))
    attn_out = bell_draw(part_keys[3], (TOKENS, HEADS * HEAD), 0.5, 4.0, ((0, 16),))
    out_grad = bell_draw(part_keys[4], (TOKENS, HEADS * HEAD), 1.0, 6.0, ((0, 16),))
    tile_doc = jnp.searchsorted(jnp.cumsum(ragged_sizes(part_keys[5], DOCS, TILES, MOST_TILES, 0)), jnp.arange(TILES), side="right").astype(jnp.int32)
    return {"queries": queries, "keys": keys, "values": values, "attn_out": attn_out, "out_grad": out_grad, "tile_doc": tile_doc}


masked_fill = -1e+30

def reference(queries, keys, values, attn_out, out_grad, tile_doc):
    score_scale = 1.0 / math.sqrt(HEAD)
    token_doc = jnp.repeat(tile_doc, TILE)
    position = jnp.arange(TOKENS, dtype=jnp.int32)
    query_block = min(512, TOKENS)
    block_count = TOKENS // query_block
    key_float = keys.astype(jnp.float32)
    value_float = values.astype(jnp.float32)

    def one_block(running, block_index):
        key_acc, value_acc = running
        first_row = (block_index * query_block).astype(jnp.int32)
        query_three = lax.dynamic_slice_in_dim(queries, first_row, query_block, 0).reshape(query_block, HEADS, HEAD).astype(jnp.float32)
        grad_three = lax.dynamic_slice_in_dim(out_grad, first_row, query_block, 0).reshape(query_block, HEADS, HEAD).astype(jnp.float32)
        out_three = lax.dynamic_slice_in_dim(attn_out, first_row, query_block, 0).reshape(query_block, HEADS, HEAD).astype(jnp.float32)
        query_pos = first_row + jnp.arange(query_block, dtype=jnp.int32)
        query_doc = lax.dynamic_slice_in_dim(token_doc, first_row, query_block, 0)
        allowed = (query_doc[:, None] == token_doc[None, :]) & (position[None, :] <= query_pos[:, None])
        scores = jnp.einsum('qhe,ke->hqk', query_three, key_float) * score_scale
        masked = jnp.where(allowed[None], scores, masked_fill)
        row_max = lax.optimization_barrier(jnp.max(masked, axis=-1, keepdims=True))
        row_sum = lax.optimization_barrier(jnp.sum(jnp.where(allowed[None], jnp.exp(masked - row_max), 0.0), axis=-1, keepdims=True))
        log_norm = row_max + jnp.log(row_sum)
        weights = jnp.where(allowed[None], jnp.exp(scores - log_norm), 0.0)
        weights_round = lax.optimization_barrier(weights.astype(jnp.bfloat16)).astype(jnp.float32)
        dprob = jnp.einsum('qhe,ke->hqk', grad_three, value_float)
        delta = jnp.transpose(lax.optimization_barrier(jnp.sum(grad_three * out_three, axis=-1)))[:, :, None]
        dscore = weights * (dprob - delta)
        dscore_round = lax.optimization_barrier(dscore.astype(jnp.bfloat16)).astype(jnp.float32)
        query_part = jnp.einsum('hqk,ke->qhe', dscore_round, key_float) * score_scale
        key_acc = key_acc + jnp.einsum('hqk,qhe->ke', dscore_round, query_three)
        value_acc = value_acc + jnp.einsum('hqk,qhe->ke', weights_round, grad_three)
        return ((key_acc, value_acc), query_part.reshape(query_block, HEADS * HEAD).astype(jnp.bfloat16))
    start_acc = (jnp.zeros((TOKENS, HEAD), jnp.float32), jnp.zeros((TOKENS, HEAD), jnp.float32))
    (key_acc, value_acc), query_parts = lax.scan(one_block, start_acc, jnp.arange(block_count, dtype=jnp.int32))
    query_grad = query_parts.reshape(TOKENS, HEADS * HEAD)
    return (query_grad, (key_acc * score_scale).astype(jnp.bfloat16), value_acc.astype(jnp.bfloat16))
```

```python
import math

import jax
import jax.numpy as jnp
from jax import lax
from jax.experimental import pallas as pl
from jax.experimental.pallas import tpu as pltpu
from jax.sharding import PartitionSpec as P

HEADS = 8
HEAD = 128
ROWS = 256
WIDE = HEADS * ROWS
RING = 8
SCALE = 1.0 / math.sqrt(HEAD)
LOG2_SCALE = SCALE * math.log2(math.e)
BIG = float(2.0**100)
OWN = 3
REACH = 12

ORDER = (
    (1, -4), (1, 3), (1, 1),
    (1, -3), (0, 4), (1, 2),
    (0, -3), (0, 3), (1, -2),
    (0, -2), (0, 2), (1, -1),
    (0, -1), (0, 1), (1, 0),
)


def slot_id(r, d):
    return d + 3 if r == 0 else d + 12


SLOTS = tuple(slot_id(r, d) for r, d in ORDER)


def dot(a, b):
    return lax.dot_general(a, b, (((1,), (0,)), ((), ())), preferred_element_type=jnp.float32)


def pick(index, values):
    out = jnp.int32(values[0])
    for i in range(1, len(values)):
        out = jnp.where(index == i, jnp.int32(values[i]), out)
    return out


def children(r, d):
    found = []
    if r == 0:
        if -3 < d <= 0:
            found.append(("up", None, (0, d - 1)))
        if 0 <= d < 4:
            found.append(("down", None, (0, d + 1)))
        if -2 <= d <= 2:
            found.append(("across", 0, (1, d)))
    else:
        if d in (-2, -3):
            found.append(("up", 1, (1, d - 1)))
        if d == 2:
            found.append(("down", 1, (1, 3)))
    return found


def kernel(
    docs, q, k, v, o, do, dq, dk, dv,
    qt, dot_, qb, dob, kall, vall, ebuf, seen, top, total, lse, dqt, pbuf, dsbuf, acck, accv, sendk, sendv, landk, landv,
    kgs, kgr, vgs, vgr, krs, krr, vrs, vrr,
):
    me = lax.axis_index("ctx")
    row = me // RING
    z = me % RING
    up = row * RING + (z + 1) % RING
    down = row * RING + (z + RING - 1) % RING
    across = (1 - row) * RING + z
    where = {"up": up, "down": down, "across": across}

    barrier = pltpu.get_barrier_semaphore()
    for other in (up, down, across):
        pl.semaphore_signal(barrier, inc=1, device_id={"ctx": other}, device_id_type=pl.DeviceIdType.MESH)

    kall[OWN] = k[...]
    vall[OWN] = v[...]
    pl.semaphore_wait(barrier, 3)

    def remote(src, dst, ssem, rsem, target):
        return pltpu.make_async_remote_copy(
            src_ref=src, dst_ref=dst, send_sem=ssem, recv_sem=rsem,
            device_id={"ctx": target}, device_id_type=pl.DeviceIdType.MESH,
        )

    gathers = ((kall, kgs, kgr), (vall, vgs, vgr))

    def only(need_row, action):
        if need_row is None:
            action()
        else:
            pl.when(row == need_row)(action)

    def forward(which, r, d):
        buf, ssem, rsem = gathers[which]
        s = slot_id(r, d)
        for direction, need_row, there in children(r, d):
            t = slot_id(*there)

            def go(direction=direction, t=t):
                remote(buf.at[s], buf.at[t], ssem.at[t], rsem.at[t], where[direction]).start()

            only(need_row, go)

    def arrived(which, r, d):
        buf, ssem, rsem = gathers[which]
        s = slot_id(r, d)

        def go():
            remote(buf.at[s], buf.at[s], ssem.at[s], rsem.at[s], up).wait_recv()

        only(None if r == 0 else 1, go)

    forward(0, 0, 0)
    forward(1, 0, 0)

    row16 = lax.broadcasted_iota(jnp.int32, (16, ROWS), 0)
    lane = lax.broadcasted_iota(jnp.int32, (ROWS, HEAD), 1)
    rowk = lax.broadcasted_iota(jnp.int32, (ROWS, HEAD), 0)
    qdoc = jnp.where(lax.broadcasted_iota(jnp.int32, (16, ROWS), 1) < 128, docs[2 * me], docs[2 * me + 1])
    mask_rows = jnp.where((row16 < 8) & (row16 != qdoc), -BIG, 0.0).astype(jnp.bfloat16)
    zeros = jnp.zeros((112, ROWS), jnp.bfloat16)
    for h in range(HEADS):
        sl = slice(h * ROWS, (h + 1) * ROWS)
        cols = slice(h * HEAD, (h + 1) * HEAD)
        qh, dh = q[:, cols], do[:, cols]
        qb[sl, :] = qh
        dob[sl, :] = dh
        qt[:HEAD, sl] = qh.T
        qt[HEAD : HEAD + 16, sl] = mask_rows
        qt[HEAD + 16 :, sl] = zeros
        dot_[:HEAD, sl] = dh.T
        prod = dh.astype(jnp.float32) * o[:, cols].astype(jnp.float32)
        minus = -jnp.sum(prod.T, axis=0, keepdims=True)
        hi = minus.astype(jnp.bfloat16).astype(jnp.float32)
        mid = (minus - hi).astype(jnp.bfloat16).astype(jnp.float32)
        low = minus - hi - mid
        rows = jnp.where(row16 == 0, hi, jnp.where(row16 == 1, mid, jnp.where(row16 == 2, low, 0.0)))
        dot_[HEAD : HEAD + 16, sl] = rows.astype(jnp.bfloat16)
        dot_[HEAD + 16 :, sl] = zeros
    dqt[...] = jnp.zeros_like(dqt)
    landk[OWN] = jnp.zeros((ROWS, HEAD), jnp.bfloat16)
    landv[OWN] = jnp.zeros((ROWS, HEAD), jnp.bfloat16)

    def block_of(s):
        far = s >= 8
        d = jnp.where(far, s - 12, s - 3)
        brow = jnp.where(far, 1 - row, row)
        return brow * RING + (z + d + RING) % RING

    def needed(s):
        b = block_of(s)
        return ((s < 8) | (row == 1)) & (b < me) & (b >= me - REACH)

    def first_pass(s, own):
        b = me if own else block_of(s)
        kdoc = jnp.where(rowk < 128, docs[2 * b], docs[2 * b + 1])
        hot = jnp.where(lane == kdoc, 1.0, 0.0).astype(jnp.bfloat16)
        ka = jnp.concatenate([kall[s], hot], axis=1)
        for h in range(HEADS):
            sl = slice(h * ROWS, (h + 1) * ROWS)
            score = dot(ka, qt[:, sl])
            if own:
                keep = lax.broadcasted_iota(jnp.int32, (ROWS, ROWS), 0) <= lax.broadcasted_iota(
                    jnp.int32, (ROWS, ROWS), 1
                )
                score = jnp.where(keep, score, -BIG)
            score = score.reshape(ROWS // 8, 8, ROWS)
            new = jnp.max(score, axis=0)
            if not own:
                old = top[:, sl]
                new = jnp.maximum(old, new)
            e = jnp.exp2((score - new[None]) * LOG2_SCALE)
            added = jnp.sum(e, axis=0)
            if not own:
                added = added + total[:, sl] * jnp.exp2((old - new) * LOG2_SCALE)
            total[:, sl] = added
            top[:, sl] = new
            seen[s, :, sl] = new
            ebuf[s, h] = e.reshape(ROWS, ROWS)

    first_pass(OWN, True)

    @pl.loop(0, 15)
    def _(step):
        for group in range(5):
            @pl.when(step == 3 * group)
            def _():
                for r, d in ORDER[12 - 3 * group : 15 - 3 * group]:
                    arrived(0, r, d)
                    forward(0, r, d)
                if group >= 1:
                    for r, d in ORDER[15 - 3 * group : 18 - 3 * group]:
                        arrived(1, r, d)
                        forward(1, r, d)

        s = pick(14 - step, SLOTS)

        @pl.when(needed(s))
        def _():
            first_pass(s, False)

    for r, d in ORDER[0:3]:
        arrived(1, r, d)

    peak = jnp.max(top[...], axis=0, keepdims=True)
    norm = jnp.sum(total[...] * jnp.exp2((top[...] - peak) * LOG2_SCALE), axis=0, keepdims=True)
    top[...] = jnp.broadcast_to(peak, (8, WIDE))
    lse[...] = jnp.broadcast_to(jnp.log2(norm), (8, WIDE))

    ones = jnp.where(lane < 3, 1.0, 0.0).astype(jnp.bfloat16)

    def stage_a(s, half):
        va = jnp.concatenate([vall[s], ones], axis=1)
        for h in range(HEADS):
            sl = slice(h * ROWS, (h + 1) * ROWS)
            inner = dot(va, dot_[:, sl])
            factor = jnp.exp2((seen[s, :, sl] - top[:, sl]) * LOG2_SCALE - lse[:, sl])
            prob = (ebuf[s, h].reshape(ROWS // 8, 8, ROWS) * factor[None]).reshape(ROWS, ROWS)
            pbuf[half, :, sl] = prob.astype(jnp.bfloat16)
            dsbuf[half, :, sl] = (prob * inner).astype(jnp.bfloat16)

    def stage_b(s, half):
        accv[...] = dot(pbuf[half], dob[...])
        acck[...] = dot(dsbuf[half], qb[...])
        dqt[...] += dot(kall[s].T, dsbuf[half])

    def following(step):
        out = jnp.int32(OWN)
        for i in reversed(range(15)):
            s = SLOTS[i]
            out = jnp.where((step < i) & needed(jnp.int32(s)), jnp.int32(s), out)
        return out

    returns = ((vall, accv, sendv, landv, vrs, vrr), (kall, acck, sendk, landk, krs, krr))

    stage_a(following(jnp.int32(-1)), 0)

    def returning(step, half):
        s = pick(step, SLOTS)
        far = s >= 8
        d = jnp.where(far, s - 12, s - 3)
        use = needed(s)

        @pl.when(use)
        def _():
            stage_a(following(step), 1 - half)
            stage_b(s, half)

        @pl.when(jnp.logical_not(use))
        def _():
            acck[...] = jnp.zeros_like(acck)
            accv[...] = jnp.zeros_like(accv)

        size = jnp.where(d < 0, -d, d)
        has_z = jnp.where(far, (d == -3) | (d == -2) | (d == 2), (d > -3) & (d < 4))
        has_y = (row == 0) & jnp.logical_not(far) & (size <= 2)
        z_from = jnp.where(has_z, jnp.where(d < 0, s - 1, s + 1), OWN)
        y_from = jnp.where(has_y, s + 9, OWN)
        target = jnp.where(far & (size <= 2), across, jnp.where(d < 0, down, up))

        @pl.when((row == 1) | jnp.logical_not(far))
        def _():
            for _, acc, out, land, ssem, rsem in returns:
                @pl.when(has_z)
                def _():
                    remote(land.at[z_from], land.at[z_from], ssem.at[z_from], rsem.at[z_from], up).wait_recv()

                @pl.when(has_y)
                def _():
                    remote(land.at[y_from], land.at[y_from], ssem.at[y_from], rsem.at[y_from], up).wait_recv()

                out[s] = (
                    acc[...] + land[z_from].astype(jnp.float32) + land[y_from].astype(jnp.float32)
                ).astype(jnp.bfloat16)
                remote(out.at[s], land.at[s], ssem.at[s], rsem.at[s], target).start()

        return jnp.where(use, 1 - half, half)

    half = lax.fori_loop(0, 15, returning, jnp.int32(0))
    stage_b(OWN, half)

    for h in range(HEADS):
        dq[:, h * HEAD : (h + 1) * HEAD] = (dqt[:, h * ROWS : (h + 1) * ROWS].T * SCALE).astype(jnp.bfloat16)

    y_from = jnp.where(row == 0, slot_id(1, 0), OWN)
    for (_, acc, out, land, ssem, rsem), result, factor in zip(returns, (dv, dk), (None, SCALE)):
        for s in (slot_id(0, -1), slot_id(0, 1)):
            remote(land.at[s], land.at[s], ssem.at[s], rsem.at[s], up).wait_recv()

        @pl.when(row == 0)
        def _():
            s = slot_id(1, 0)
            remote(land.at[s], land.at[s], ssem.at[s], rsem.at[s], up).wait_recv()

        whole = acc[...]
        for s in (slot_id(0, -1), slot_id(0, 1), y_from):
            whole = whole + land[s].astype(jnp.float32)
        if factor is not None:
            whole = whole * factor
        result[...] = whole.astype(jnp.bfloat16)

    for r, d in ORDER + ((0, 0),):
        for which in range(2):
            buf, ssem, rsem = gathers[which]
            for direction, need_row, there in children(r, d):
                t = slot_id(*there)

                def go(t=t):
                    remote(buf.at[t], buf.at[t], ssem.at[t], rsem.at[t], up).wait_send()

                only(need_row, go)
    for r, d in ORDER:
        s = slot_id(r, d)
        for _, acc, out, land, ssem, rsem in returns:

            def go():
                remote(out.at[s], land.at[s], ssem.at[s], rsem.at[s], up).wait_send()

            only(None if r == 0 else 1, go)


def local(queries, keys, values, attn_out, out_grad, tile_doc):
    vmem = pl.BlockSpec(memory_space=pltpu.VMEM)
    bf16, f32 = jnp.bfloat16, jnp.float32
    return pl.pallas_call(
        kernel,
        out_shape=(
            jax.ShapeDtypeStruct((ROWS, HEADS * HEAD), bf16),
            jax.ShapeDtypeStruct((ROWS, HEAD), bf16),
            jax.ShapeDtypeStruct((ROWS, HEAD), bf16),
        ),
        in_specs=[pl.BlockSpec(memory_space=pltpu.SMEM)] + [vmem] * 5,
        out_specs=(vmem, vmem, vmem),
        scratch_shapes=[
            pltpu.VMEM((2 * HEAD, WIDE), bf16),
            pltpu.VMEM((2 * HEAD, WIDE), bf16),
            pltpu.VMEM((WIDE, HEAD), bf16),
            pltpu.VMEM((WIDE, HEAD), bf16),
            pltpu.VMEM((16, ROWS, HEAD), bf16),
            pltpu.VMEM((16, ROWS, HEAD), bf16),
            pltpu.VMEM((16, HEADS, ROWS, ROWS), f32),
            pltpu.VMEM((16, 8, WIDE), f32),
            pltpu.VMEM((8, WIDE), f32),
            pltpu.VMEM((8, WIDE), f32),
            pltpu.VMEM((8, WIDE), f32),
            pltpu.VMEM((HEAD, WIDE), f32),
            pltpu.VMEM((2, ROWS, WIDE), bf16),
            pltpu.VMEM((2, ROWS, WIDE), bf16),
            pltpu.VMEM((ROWS, HEAD), f32),
            pltpu.VMEM((ROWS, HEAD), f32),
            pltpu.VMEM((16, ROWS, HEAD), bf16),
            pltpu.VMEM((16, ROWS, HEAD), bf16),
            pltpu.VMEM((16, ROWS, HEAD), bf16),
            pltpu.VMEM((16, ROWS, HEAD), bf16),
        ]
        + [pltpu.SemaphoreType.DMA((16,))] * 8,
        compiler_params=pltpu.CompilerParams(
            collective_id=0, has_side_effects=True, vmem_limit_bytes=60 * 2**20
        ),
        name="attention_backward",
    )(tile_doc, queries, keys, values, attn_out, out_grad)


def solution(mesh):
    rows = P(("seq", "ctx"), None)
    return jax.shard_map(
        local,
        mesh=mesh,
        in_specs=(rows, rows, rows, rows, rows, P("seq")),
        out_specs=(rows, rows, rows),
        check_vma=False,
    )
```

```python
import math

import jax
import jax.numpy as jnp
from jax import lax
from jax.experimental import pallas as pl
from jax.experimental.pallas import tpu as pltpu
from jax.sharding import PartitionSpec as P

HEADS = 8
HEAD = 128
ROWS = 256
WIDE = HEADS * ROWS
RING = 8
SCALE = 1.0 / math.sqrt(HEAD)
LOG2_SCALE = SCALE * math.log2(math.e)
BIG = float(2.0**100)
OWN = 3
REACH = 12

ORDER = (
    (0, -1), (1, 0), (0, 1), (0, -2), (0, 2),
    (1, -1), (1, 1), (1, -2), (1, 2),
    (0, -3), (0, 3), (1, -3), (1, 3),
    (0, 4), (1, 4),
)
BACK = (
    (1, 0), (0, -1), (0, 1), (1, -1),
    (1, 4), (0, 4), (1, 3), (1, -3), (0, 3), (0, -3), (1, 2), (1, -2), (1, 1), (0, 2), (0, -2),
)
SENDS = tuple([(3, (1, -1))] + [(n, BACK[n]) for n in range(4, 15)] + [(14, x) for x in BACK[:3]])
BOTH, ROW0, ROW1 = (0, 1), (0,), (1,)
ARRIVALS = (
    ((ROW0, (0, -2)), (ROW0, (0, 2)), (BOTH, (0, -1)), (BOTH, (0, 1)), (ROW1, (1, 0))),
    ((ROW1, (1, -2)), (ROW1, (1, 2)), (BOTH, (0, -3), 0), (BOTH, (0, 3), 0), (ROW1, (0, -2)), (ROW1, (0, 2)),
     (ROW1, (1, -1)), (ROW1, (1, 1))),
    ((ROW1, (1, -3)), (ROW1, (1, 3)), (ROW1, (0, -3)), (ROW1, (0, 3)), (ROW0, (0, 4))),
    ((ROW1, (0, 4)), (ROW1, (1, 4))),
)
KEY_STEPS = (0, 3, 9, 13)
VALUE_STEPS = (5, 10, 14, None)
LAST_VALUES = 2


def slot_id(r, d):
    return d + 3 if r == 0 else d + 11


SLOTS = tuple(slot_id(r, d) for r, d in ORDER)

RAW_EDGES = (
    ((0, -1), (0, 0), 1, 0, lambda r, z: True),
    ((0, -2), (0, 0), 2, 0, lambda r, z: r == 0),
    ((0, 1), (0, 0), -1, 0, lambda r, z: True),
    ((0, 2), (0, 0), -2, 0, lambda r, z: r == 0),
    ((1, 0), (0, 0), 0, 1, lambda r, z: r == 1),
    ((0, -2), (0, -1), 1, 0, lambda r, z: r == 1),
    ((0, 2), (0, 1), -1, 0, lambda r, z: r == 1),
    ((1, -2), (0, -2), 0, 1, lambda r, z: r == 1),
    ((1, 2), (0, 2), 0, 1, lambda r, z: r == 1),
    ((1, -1), (0, -1), 0, 1, lambda r, z: r == 1),
    ((1, 1), (1, 0), -1, 0, lambda r, z: r == 1),
    ((0, -3), (0, -2), 1, 0, lambda r, z: True),
    ((0, 3), (0, 2), -1, 0, lambda r, z: True),
    ((1, -3), (0, -3), 0, 1, lambda r, z: r == 1 and z >= 3),
    ((1, -3), (1, -2), 1, 0, lambda r, z: r == 1 and z < 3),
    ((1, 3), (1, 2), -1, 0, lambda r, z: r == 1),
    ((0, 4), (0, -3), 1, 0, lambda r, z: True),
    ((1, 4), (1, -3), 1, 0, lambda r, z: r == 1 and 4 <= z < 7),
    ((1, 4), (0, 4), 0, 1, lambda r, z: r == 1 and z == 7),
    ((1, 4), (1, 3), -1, 0, lambda r, z: r == 1 and z < 4),
)


def plan():
    masks = [0] * len(RAW_EDGES)
    todo = []
    for me in range(2 * RING):
        row, z = divmod(me, RING)
        for r, d in ORDER:
            block = (row if r == 0 else 1 - row) * RING + (z + d) % RING
            if me - REACH <= block < me:
                todo.append((row, z, (r, d)))
    while todo:
        row, z, slot = todo.pop()
        if slot == (0, 0):
            continue
        found = [n for n, edge in enumerate(RAW_EDGES) if edge[0] == slot and edge[4](row, z)]
        assert len(found) == 1, (row, z, slot)
        bit = 1 << (row * RING + z)
        if not masks[found[0]] & bit:
            masks[found[0]] |= bit
            _, parent, dz, dy, _ = RAW_EDGES[found[0]]
            todo.append((row ^ dy, (z - dz) % RING, parent))
    return masks


MASKS = plan()
NEEDED = tuple(
    sum(
        1 << me
        for me in range(2 * RING)
        if me - REACH <= (me // RING ^ r) * RING + (me % RING + d) % RING < me
    )
    for r, d in ORDER
)
EDGES = tuple((slot_id(*t), slot_id(*p), dz, dy) for t, p, dz, dy, _ in RAW_EDGES)
NEED_MASKS = dict(zip(SLOTS, NEEDED))
SLOT_MASKS = {s: sum(m for m, e in zip(MASKS, EDGES) if e[0] == s) for s in range(16)}


def dot(a, b):
    return lax.dot_general(a, b, (((1,), (0,)), ((), ())), preferred_element_type=jnp.float32)


def pick(index, values):
    out = jnp.int32(values[0])
    for i in range(1, len(values)):
        out = jnp.where(index == i, jnp.int32(values[i]), out)
    return out


def kernel(
    docs, q_any, k, v, o_any, do_any, dq_any, dk, dv,
    q, o, do, dq, qt, dot_, qb, dob, kall, vall, ebuf, seen, top, total, lse, dqt, pbuf, dsbuf, acck, accv,
    sendk, sendv, landk, landv, kgs, kgr, vgs, vgr, krs, krr, vrs, vrr, here,
):
    me = lax.axis_index("ctx")
    row = me // RING
    z = me % RING

    def place(dz, dy):
        other = 1 - row if dy else row
        return other * RING + (z + dz + RING) % RING

    def in_mask(mask, device):
        return (jnp.int32(mask) >> device) & 1 == 1

    near = [(1, 0), (-1, 0), (2, 0), (-2, 0), (0, 1)]
    barrier = pltpu.get_barrier_semaphore()
    for dz, dy in near:
        pl.semaphore_signal(barrier, inc=1, device_id={"ctx": place(dz, dy)}, device_id_type=pl.DeviceIdType.MESH)

    loads = [
        pltpu.make_async_copy(src, dst, here.at[n])
        for n, (src, dst) in enumerate(((q_any, q), (do_any, do), (o_any, o)))
    ]
    for load in loads:
        load.start()
    kall[OWN] = k[...]
    vall[OWN] = v[...]
    pl.semaphore_wait(barrier, len(near))

    def remote(src, dst, ssem, rsem, target):
        return pltpu.make_async_remote_copy(
            src_ref=src, dst_ref=dst, send_sem=ssem, recv_sem=rsem,
            device_id={"ctx": target}, device_id_type=pl.DeviceIdType.MESH,
        )

    gathers = ((kall, kgs, kgr), (vall, vgs, vgr))

    def forward(which, s):
        buf, ssem, rsem = gathers[which]
        for n, (t, parent, dz, dy) in enumerate(EDGES):
            if parent == s and MASKS[n]:
                target = place(dz, dy)

                @pl.when(in_mask(MASKS[n], target))
                def _(n=n, t=t, target=target):
                    remote(buf.at[s], buf.at[t], ssem.at[n], rsem.at[t], target).start()

    def arrive(which, stage):
        buf, _, rsem = gathers[which]
        for rows, (r, d), *only in ARRIVALS[stage]:
            s = slot_id(r, d)
            mask = SLOT_MASKS[s] & sum(0xFF << (RING * n) for n in (only or rows))
            if mask:

                @pl.when(in_mask(mask, me))
                def _(s=s):
                    remote(buf.at[s], buf.at[s], here.at[0], rsem.at[s], me).wait_recv()
                    forward(which, s)

    forward(0, OWN)
    for load in loads:
        load.wait()

    row16 = lax.broadcasted_iota(jnp.int32, (16, ROWS), 0)
    lane = lax.broadcasted_iota(jnp.int32, (ROWS, HEAD), 1)
    rowk = lax.broadcasted_iota(jnp.int32, (ROWS, HEAD), 0)
    qdoc = jnp.where(lax.broadcasted_iota(jnp.int32, (16, ROWS), 1) < 128, docs[2 * me], docs[2 * me + 1])
    mask_rows = jnp.where((row16 < 8) & (row16 != qdoc), -BIG, 0.0).astype(jnp.bfloat16)
    zeros = jnp.zeros((112, ROWS), jnp.bfloat16)
    for h in range(HEADS):
        sl = slice(h * ROWS, (h + 1) * ROWS)
        cols = slice(h * HEAD, (h + 1) * HEAD)
        qh, dh = q[:, cols], do[:, cols]
        qb[sl, :] = qh
        dob[sl, :] = dh
        qt[:HEAD, sl] = qh.T
        qt[HEAD : HEAD + 16, sl] = mask_rows
        qt[HEAD + 16 :, sl] = zeros
        dot_[:HEAD, sl] = dh.T
        prod = dh.astype(jnp.float32) * o[:, cols].astype(jnp.float32)
        minus = -jnp.sum(prod.T, axis=0, keepdims=True)
        hi = minus.astype(jnp.bfloat16).astype(jnp.float32)
        mid = (minus - hi).astype(jnp.bfloat16).astype(jnp.float32)
        low = minus - hi - mid
        rows = jnp.where(row16 == 0, hi, jnp.where(row16 == 1, mid, jnp.where(row16 == 2, low, 0.0)))
        dot_[HEAD : HEAD + 16, sl] = rows.astype(jnp.bfloat16)
        dot_[HEAD + 16 :, sl] = zeros
    dqt[...] = jnp.zeros_like(dqt)

    def block_of(s):
        far = s >= 8
        d = jnp.where(far, s - 11, s - 3)
        brow = jnp.where(far, 1 - row, row)
        return brow * RING + (z + d + RING) % RING

    def first_pass(s, own):
        b = me if own else block_of(s)
        kdoc = jnp.where(rowk < 128, docs[2 * b], docs[2 * b + 1])
        hot = jnp.where(lane == kdoc, 1.0, 0.0).astype(jnp.bfloat16)
        ka = jnp.concatenate([kall[s], hot], axis=1)
        for h in range(HEADS):
            sl = slice(h * ROWS, (h + 1) * ROWS)
            score = dot(ka, qt[:, sl])
            if own:
                keep = lax.broadcasted_iota(jnp.int32, (ROWS, ROWS), 0) <= lax.broadcasted_iota(
                    jnp.int32, (ROWS, ROWS), 1
                )
                score = jnp.where(keep, score, -BIG)
            score = score.reshape(ROWS // 8, 8, ROWS)
            new = jnp.max(score, axis=0)
            if not own:
                old = top[:, sl]
                new = jnp.maximum(old, new)
            e = jnp.exp2((score - new[None]) * LOG2_SCALE)
            added = jnp.sum(e, axis=0)
            if not own:
                added = added + total[:, sl] * jnp.exp2((old - new) * LOG2_SCALE)
            total[:, sl] = added
            top[:, sl] = new
            seen[s, :, sl] = new
            ebuf[s, h] = e.reshape(ROWS, ROWS)

    first_pass(OWN, True)

    @pl.loop(0, 15)
    def _(step):
        for stage in range(4):
            for which, steps in ((0, KEY_STEPS), (1, VALUE_STEPS)):
                if steps[stage] is not None:

                    @pl.when(step == steps[stage])
                    def _(which=which, stage=stage):
                        arrive(which, stage)
                        if which == 0 and stage == 0:
                            forward(1, OWN)

        @pl.when(in_mask(pick(step, NEEDED), me))
        def _():
            first_pass(pick(step, SLOTS), False)

    peak = jnp.max(top[...], axis=0, keepdims=True)
    norm = jnp.sum(total[...] * jnp.exp2((top[...] - peak) * LOG2_SCALE), axis=0, keepdims=True)
    top[...] = jnp.broadcast_to(peak, (8, WIDE))
    lse[...] = jnp.broadcast_to(jnp.log2(norm), (8, WIDE))

    ones = jnp.where(lane < 3, 1.0, 0.0).astype(jnp.bfloat16)

    def stage_a(s, half):
        va = jnp.concatenate([vall[s], ones], axis=1)
        for h in range(HEADS):
            sl = slice(h * ROWS, (h + 1) * ROWS)
            inner = dot(va, dot_[:, sl])
            factor = jnp.exp2((seen[s, :, sl] - top[:, sl]) * LOG2_SCALE - lse[:, sl])
            prob = (ebuf[s, h].reshape(ROWS // 8, 8, ROWS) * factor[None]).reshape(ROWS, ROWS)
            pbuf[half, :, sl] = prob.astype(jnp.bfloat16)
            dsbuf[half, :, sl] = (prob * inner).astype(jnp.bfloat16)

    def stage_b(s, half):
        accv[s] = dot(pbuf[half], dob[...])
        acck[s] = dot(dsbuf[half], qb[...])
        dqt[...] += dot(kall[s].T, dsbuf[half])

    back = tuple(slot_id(r, d) for r, d in BACK)

    def following(step):
        out = jnp.int32(OWN)
        for i in reversed(range(15)):
            out = jnp.where((step < i) & in_mask(NEED_MASKS[back[i]], me), jnp.int32(back[i]), out)
        return out

    returns = ((accv, sendv, landv, vrs, vrr), (acck, sendk, landk, krs, krr))

    def add_children(s):
        for acc, out, land, ssem, rsem in returns:
            for n, (t, parent, dz, dy) in enumerate(EDGES):
                if parent == s and MASKS[n]:

                    @pl.when(in_mask(MASKS[n], place(dz, dy)))
                    def _(n=n):
                        remote(land.at[n], land.at[n], ssem.at[n], rsem.at[n], me).wait_recv()
                        acc[s] += land[n].astype(jnp.float32)

            if s == OWN:
                continue
            out[s] = acc[s].astype(jnp.bfloat16)
            for n, (t, parent, dz, dy) in enumerate(EDGES):
                if t == s and MASKS[n]:

                    @pl.when(in_mask(MASKS[n], me))
                    def _(n=n, dz=dz, dy=dy):
                        remote(out.at[s], land.at[n], ssem.at[n], rsem.at[n], place(-dz, dy)).start()

    for s in SLOTS:
        relay = SLOT_MASKS[s] & ~NEED_MASKS[s]
        if relay:

            @pl.when(in_mask(relay, me))
            def _(s=s):
                acck[s] = jnp.zeros((ROWS, HEAD), jnp.float32)
                accv[s] = jnp.zeros((ROWS, HEAD), jnp.float32)

    stage_a(following(jnp.int32(-1)), 0)

    def returning(step, half):
        use = in_mask(pick(step, tuple(NEED_MASKS[s] for s in back)), me)

        @pl.when(step == LAST_VALUES)
        def _():
            arrive(1, 3)

        @pl.when(use)
        def _():
            stage_a(following(step), 1 - half)
            stage_b(pick(step, back), half)

        for n, slot in SENDS:
            s = slot_id(*slot)

            @pl.when((step == n) & in_mask(SLOT_MASKS[s], me))
            def _(s=s):
                add_children(s)

        return jnp.where(use, 1 - half, half)

    half = lax.fori_loop(0, 15, returning, jnp.int32(0))
    stage_b(OWN, half)

    for h in range(HEADS):
        dq[:, h * HEAD : (h + 1) * HEAD] = (dqt[:, h * ROWS : (h + 1) * ROWS].T * SCALE).astype(jnp.bfloat16)
    store = pltpu.make_async_copy(dq, dq_any, here.at[0])
    store.start()
    add_children(OWN)
    dv[...] = accv[OWN].astype(jnp.bfloat16)
    dk[...] = (acck[OWN] * SCALE).astype(jnp.bfloat16)

    for n, (t, parent, dz, dy) in enumerate(EDGES):
        if MASKS[n]:

            @pl.when(in_mask(MASKS[n], place(dz, dy)))
            def _(n=n):
                for buf, ssem, rsem in gathers:
                    remote(buf.at[0], buf.at[0], ssem.at[n], rsem.at[0], me).wait_send()

            @pl.when(in_mask(MASKS[n], me))
            def _(n=n):
                for _, out, land, ssem, rsem in returns:
                    remote(out.at[0], land.at[n], ssem.at[n], rsem.at[n], me).wait_send()

    store.wait()


def hand_over(dq, dk, dv, dq_out, dk_out, dv_out):
    dq_out[...] = dq[...]
    dk_out[...] = dk[...]
    dv_out[...] = dv[...]


def local(queries, keys, values, attn_out, out_grad, tile_doc):
    vmem = pl.BlockSpec(memory_space=pltpu.VMEM)
    bf16, f32 = jnp.bfloat16, jnp.float32
    any_ = pl.BlockSpec(memory_space=pl.ANY)
    shapes = (
        jax.ShapeDtypeStruct((ROWS, HEADS * HEAD), bf16),
        jax.ShapeDtypeStruct((ROWS, HEAD), bf16),
        jax.ShapeDtypeStruct((ROWS, HEAD), bf16),
    )
    results = pl.pallas_call(
        kernel,
        out_shape=shapes,
        in_specs=[pl.BlockSpec(memory_space=pltpu.SMEM), any_, vmem, vmem, any_, any_],
        out_specs=(any_, vmem, vmem),
        scratch_shapes=[pltpu.VMEM((ROWS, HEADS * HEAD), bf16)] * 4
        + [
            pltpu.VMEM((2 * HEAD, WIDE), bf16),
            pltpu.VMEM((2 * HEAD, WIDE), bf16),
            pltpu.VMEM((WIDE, HEAD), bf16),
            pltpu.VMEM((WIDE, HEAD), bf16),
            pltpu.VMEM((16, ROWS, HEAD), bf16),
            pltpu.VMEM((16, ROWS, HEAD), bf16),
            pltpu.VMEM((16, HEADS, ROWS, ROWS), f32),
            pltpu.VMEM((16, 8, WIDE), f32),
            pltpu.VMEM((8, WIDE), f32),
            pltpu.VMEM((8, WIDE), f32),
            pltpu.VMEM((8, WIDE), f32),
            pltpu.VMEM((HEAD, WIDE), f32),
            pltpu.VMEM((2, ROWS, WIDE), bf16),
            pltpu.VMEM((2, ROWS, WIDE), bf16),
            pltpu.VMEM((16, ROWS, HEAD), f32),
            pltpu.VMEM((16, ROWS, HEAD), f32),
            pltpu.VMEM((16, ROWS, HEAD), bf16),
            pltpu.VMEM((16, ROWS, HEAD), bf16),
            pltpu.VMEM((len(EDGES), ROWS, HEAD), bf16),
            pltpu.VMEM((len(EDGES), ROWS, HEAD), bf16),
        ]
        + [pltpu.SemaphoreType.DMA((len(EDGES),))] * 8
        + [pltpu.SemaphoreType.DMA((3,))],
        compiler_params=pltpu.CompilerParams(
            collective_id=0, has_side_effects=True, vmem_limit_bytes=60 * 2**20
        ),
        name="attention_backward",
    )(tile_doc, queries, keys, values, attn_out, out_grad)
    return pl.pallas_call(
        hand_over,
        out_shape=shapes,
        in_specs=[vmem] * 3,
        out_specs=(vmem,) * 3,
        name="hand_over",
    )(*results)


def solution(mesh):
    rows = P(("seq", "ctx"), None)
    return jax.shard_map(
        local,
        mesh=mesh,
        in_specs=(rows, rows, rows, rows, rows, P("seq")),
        out_specs=(rows, rows, rows),
        check_vma=False,
    )
```

```python
import math

import jax
import jax.numpy as jnp
from jax import lax
from jax.experimental import pallas as pl
from jax.experimental.pallas import tpu as pltpu
from jax.sharding import PartitionSpec as P

HEADS = 8
HEAD = 128
ROWS = 256
WIDE = HEADS * ROWS
RING = 8
SCALE = 1.0 / math.sqrt(HEAD)
LOG2_SCALE = SCALE * math.log2(math.e)
BIG = float(2.0**100)
OWN = 3
REACH = 12

ORDER = (
    (0, -1), (1, 0), (0, 1), (0, -2), (0, 2),
    (1, -1), (1, 1), (1, -2), (1, 2), (0, -3), (0, 3),
    (1, -3), (1, 3), (0, 4), (1, 4),
)
BACK = (
    (1, -1), (1, -2), (1, 4), (0, 4), (1, -3), (1, 3), (1, 1), (0, 3), (0, -3), (1, 2),
    (0, 2), (0, 1), (0, -2), (0, -1), (1, 0),
)
SENDS = {
    (1, -1): (0, 0), (1, 4): (2, 2), (0, 4): (3, 3), (1, -3): (4, 4), (1, 3): (5, 5), (1, 1): (6, 6), (0, 3): (7, 7),
    (0, -3): (8, 8), (1, -2): (8, 8), (1, 2): (10, 10), (0, 2): (13, 11), (0, 1): (11, 11), (0, -2): (13, 13),
    (0, -1): (13, 13), (1, 0): (14, 14),
}
ARRIVALS = (
    ((0, -2), (0, 2), (0, -1), (0, 1), (1, 0)),
    ((1, -2), (1, 2), (0, -3), (0, 3), (1, -1), (1, 1)),
    ((1, -3), (1, 3), (0, 4), (1, 4)),
)
KEY_STEPS = (0, 3, 9)
VALUE_STEPS = (3, 9)


def slot_id(r, d):
    return d + 3 if r == 0 else d + 11


SLOTS = tuple(slot_id(r, d) for r, d in ORDER)

RAW_EDGES = (
    ((0, -2), (0, 0), 2, 0, lambda r, z: True),
    ((0, 2), (0, 0), -2, 0, lambda r, z: True),
    ((0, -1), (0, 0), 1, 0, lambda r, z: True),
    ((0, 1), (0, 0), -1, 0, lambda r, z: True),
    ((1, 0), (0, 0), 0, 1, lambda r, z: r == 1),
    ((1, -2), (0, -2), 0, 1, lambda r, z: r == 1),
    ((1, 2), (0, 2), 0, 1, lambda r, z: r == 1),
    ((1, -1), (0, -1), 0, 1, lambda r, z: r == 1),
    ((1, 1), (1, 0), -1, 0, lambda r, z: r == 1),
    ((0, -3), (0, -2), 1, 0, lambda r, z: True),
    ((0, 3), (0, 2), -1, 0, lambda r, z: True),
    ((1, -3), (0, -3), 0, 1, lambda r, z: r == 1 and z >= 3),
    ((1, -3), (1, -2), 1, 0, lambda r, z: r == 1 and z < 3),
    ((1, 3), (1, 2), -1, 0, lambda r, z: r == 1),
    ((0, 4), (0, -3), 1, 0, lambda r, z: True),
    ((1, 4), (1, -2), 2, 0, lambda r, z: r == 1 and z >= 4),
    ((1, 4), (1, 2), -2, 0, lambda r, z: r == 1 and z < 4),
)
HALF_EDGE = 15


def plan():
    masks = [0] * len(RAW_EDGES)
    todo = []
    for me in range(2 * RING):
        row, z = divmod(me, RING)
        for r, d in ORDER:
            block = (row if r == 0 else 1 - row) * RING + (z + d) % RING
            if me - REACH <= block < me:
                todo.append((row, z, (r, d)))
    while todo:
        row, z, slot = todo.pop()
        if slot == (0, 0):
            continue
        found = [n for n, edge in enumerate(RAW_EDGES) if edge[0] == slot and edge[4](row, z)]
        assert len(found) == 1, (row, z, slot)
        bit = 1 << (row * RING + z)
        if not masks[found[0]] & bit:
            masks[found[0]] |= bit
            _, parent, dz, dy, _ = RAW_EDGES[found[0]]
            todo.append((row ^ dy, (z - dz) % RING, parent))
    return masks


MASKS = plan()
NEEDED = tuple(
    sum(
        1 << me
        for me in range(2 * RING)
        if me - REACH <= (me // RING ^ r) * RING + (me % RING + d) % RING < me
    )
    for r, d in ORDER
)
EDGES = tuple((slot_id(*t), slot_id(*p), dz, dy) for t, p, dz, dy, _ in RAW_EDGES)
for child, parent, _, _, _ in RAW_EDGES:
    assert parent == (0, 0) or all(a < b for a in SENDS[child] for b in SENDS[parent])
NEED_MASKS = dict(zip(SLOTS, NEEDED))
SLOT_MASKS = {s: sum(m for m, e in zip(MASKS, EDGES) if e[0] == s) for s in range(16)}


def dot(a, b):
    return lax.dot_general(a, b, (((1,), (0,)), ((), ())), preferred_element_type=jnp.float32)


def pick(index, values):
    out = jnp.int32(values[0])
    for i in range(1, len(values)):
        out = jnp.where(index == i, jnp.int32(values[i]), out)
    return out


def kernel(
    docs, q_any, k, v, o_any, do_any, dq_any, dk, dv,
    q, o, do, dq, qt, dot_, qb, dob, kall, vall, ebuf, seen, top, total, lse, dqt, pbuf, dsbuf, acck, accv,
    sendk, sendv, landk, landv, kgs, kgr, vgs, vgr, krs, krr, vrs, vrr, here,
):
    me = lax.axis_index("ctx")
    row = me // RING
    z = me % RING

    def place(dz, dy):
        other = 1 - row if dy else row
        return other * RING + (z + dz + RING) % RING

    def in_mask(mask, device):
        return (jnp.int32(mask) >> device) & 1 == 1

    near = [(1, 0), (-1, 0), (2, 0), (-2, 0), (0, 1)]
    barrier = pltpu.get_barrier_semaphore()
    for dz, dy in near:
        pl.semaphore_signal(barrier, inc=1, device_id={"ctx": place(dz, dy)}, device_id_type=pl.DeviceIdType.MESH)

    loads = [
        pltpu.make_async_copy(src, dst, here.at[n])
        for n, (src, dst) in enumerate(((q_any, q), (do_any, do), (o_any, o)))
    ]
    for load in loads:
        load.start()
    kall[OWN] = k[...]
    vall[OWN] = v[...]

    @pl.when(in_mask(MASKS[HALF_EDGE], me))
    def _():
        kall[EDGES[HALF_EDGE][0], : ROWS // 2] = jnp.zeros((ROWS // 2, HEAD), jnp.bfloat16)
        vall[EDGES[HALF_EDGE][0], : ROWS // 2] = jnp.zeros((ROWS // 2, HEAD), jnp.bfloat16)

    pl.semaphore_wait(barrier, len(near))

    def remote(src, dst, ssem, rsem, target):
        return pltpu.make_async_remote_copy(
            src_ref=src, dst_ref=dst, send_sem=ssem, recv_sem=rsem,
            device_id={"ctx": target}, device_id_type=pl.DeviceIdType.MESH,
        )

    def rows_of(n):
        return pl.ds(ROWS // 2, ROWS // 2) if n == HALF_EDGE else pl.ds(0, ROWS)

    gathers = ((kall, kgs, kgr), (vall, vgs, vgr))

    def forward(which, s):
        buf, ssem, rsem = gathers[which]
        for n, (t, parent, dz, dy) in enumerate(EDGES):
            if parent == s and MASKS[n]:
                target = place(dz, dy)

                @pl.when(in_mask(MASKS[n], target))
                def _(n=n, t=t, target=target):
                    part = rows_of(n)
                    remote(buf.at[s, part], buf.at[t, part], ssem.at[n], rsem.at[t], target).start()

    def arrive(which, stage):
        buf, _, rsem = gathers[which]
        for r, d in ARRIVALS[stage]:
            s = slot_id(r, d)
            for n, edge in enumerate(EDGES):
                if edge[0] == s and MASKS[n]:

                    @pl.when(in_mask(MASKS[n], me))
                    def _(n=n):
                        part = rows_of(n)
                        remote(buf.at[s, part], buf.at[s, part], here.at[0], rsem.at[s], me).wait_recv()

            if SLOT_MASKS[s]:

                @pl.when(in_mask(SLOT_MASKS[s], me))
                def _(s=s):
                    forward(which, s)

    forward(0, OWN)
    forward(1, OWN)
    for load in loads:
        load.wait()

    row16 = lax.broadcasted_iota(jnp.int32, (16, ROWS), 0)
    lane = lax.broadcasted_iota(jnp.int32, (ROWS, HEAD), 1)
    rowk = lax.broadcasted_iota(jnp.int32, (ROWS, HEAD), 0)
    qdoc = jnp.where(lax.broadcasted_iota(jnp.int32, (16, ROWS), 1) < 128, docs[2 * me], docs[2 * me + 1])
    mask_rows = jnp.where((row16 < 8) & (row16 != qdoc), -BIG, 0.0).astype(jnp.bfloat16)
    zeros = jnp.zeros((112, ROWS), jnp.bfloat16)
    for h in range(HEADS):
        sl = slice(h * ROWS, (h + 1) * ROWS)
        cols = slice(h * HEAD, (h + 1) * HEAD)
        qh, dh = q[:, cols], do[:, cols]
        qb[sl, :] = qh
        dob[sl, :] = dh
        qt[:HEAD, sl] = qh.T
        qt[HEAD : HEAD + 16, sl] = mask_rows
        qt[HEAD + 16 :, sl] = zeros
        dot_[:HEAD, sl] = dh.T
        prod = dh.astype(jnp.float32) * o[:, cols].astype(jnp.float32)
        minus = -jnp.sum(prod.T, axis=0, keepdims=True)
        hi = minus.astype(jnp.bfloat16).astype(jnp.float32)
        mid = (minus - hi).astype(jnp.bfloat16).astype(jnp.float32)
        low = minus - hi - mid
        rows = jnp.where(row16 == 0, hi, jnp.where(row16 == 1, mid, jnp.where(row16 == 2, low, 0.0)))
        dot_[HEAD : HEAD + 16, sl] = rows.astype(jnp.bfloat16)
        dot_[HEAD + 16 :, sl] = zeros
    dqt[...] = jnp.zeros_like(dqt)

    def block_of(s):
        far = s >= 8
        d = jnp.where(far, s - 11, s - 3)
        brow = jnp.where(far, 1 - row, row)
        return brow * RING + (z + d + RING) % RING

    def first_pass(s, own):
        b = me if own else block_of(s)
        kdoc = jnp.where(rowk < 128, docs[2 * b], docs[2 * b + 1])
        hot = jnp.where(lane == kdoc, 1.0, 0.0).astype(jnp.bfloat16)
        ka = jnp.concatenate([kall[s], hot], axis=1)
        for h in range(HEADS):
            sl = slice(h * ROWS, (h + 1) * ROWS)
            score = dot(ka, qt[:, sl])
            if own:
                keep = lax.broadcasted_iota(jnp.int32, (ROWS, ROWS), 0) <= lax.broadcasted_iota(
                    jnp.int32, (ROWS, ROWS), 1
                )
                score = jnp.where(keep, score, -BIG)
            score = score.reshape(ROWS // 8, 8, ROWS)
            new = jnp.max(score, axis=0)
            if not own:
                old = top[:, sl]
                new = jnp.maximum(old, new)
            e = jnp.exp2((score - new[None]) * LOG2_SCALE)
            added = jnp.sum(e, axis=0)
            if not own:
                added = added + total[:, sl] * jnp.exp2((old - new) * LOG2_SCALE)
            total[:, sl] = added
            top[:, sl] = new
            seen[s, :, sl] = new
            ebuf[s, h] = e.reshape(ROWS, ROWS)

    first_pass(OWN, True)

    @pl.loop(0, 15)
    def _(step):
        for n in range(15):
            due = [(w, i) for w, steps in ((0, KEY_STEPS), (1, VALUE_STEPS)) for i, at in enumerate(steps) if at == n]
            if due:

                @pl.when(step == n)
                def _(due=due):
                    for which, stage in due:
                        arrive(which, stage)

        @pl.when(in_mask(pick(step, NEEDED), me))
        def _():
            first_pass(pick(step, SLOTS), False)

    peak = jnp.max(top[...], axis=0, keepdims=True)
    norm = jnp.sum(total[...] * jnp.exp2((top[...] - peak) * LOG2_SCALE), axis=0, keepdims=True)
    top[...] = jnp.broadcast_to(peak, (8, WIDE))
    lse[...] = jnp.broadcast_to(jnp.log2(norm), (8, WIDE))

    ones = jnp.where(lane < 3, 1.0, 0.0).astype(jnp.bfloat16)

    def stage_a(s, half):
        va = jnp.concatenate([vall[s], ones], axis=1)
        for h in range(HEADS):
            sl = slice(h * ROWS, (h + 1) * ROWS)
            inner = dot(va, dot_[:, sl])
            factor = jnp.exp2((seen[s, :, sl] - top[:, sl]) * LOG2_SCALE - lse[:, sl])
            prob = (ebuf[s, h].reshape(ROWS // 8, 8, ROWS) * factor[None]).reshape(ROWS, ROWS)
            pbuf[half, :, sl] = prob.astype(jnp.bfloat16)
            dsbuf[half, :, sl] = (prob * inner).astype(jnp.bfloat16)

    def stage_b(s, half):
        accv[s] = dot(pbuf[half], dob[...])
        acck[s] = dot(dsbuf[half], qb[...])
        dqt[...] += dot(kall[s].T, dsbuf[half])

    back = tuple(slot_id(r, d) for r, d in BACK)

    def following(step):
        out = jnp.int32(OWN)
        for i in reversed(range(15)):
            out = jnp.where((step < i) & in_mask(NEED_MASKS[back[i]], me), jnp.int32(back[i]), out)
        return out

    returns = ((accv, sendv, landv, vrs, vrr), (acck, sendk, landk, krs, krr))

    def add_children(s):
        for acc, out, land, ssem, rsem in returns:
            for n, (t, parent, dz, dy) in enumerate(EDGES):
                if parent == s and MASKS[n]:

                    @pl.when(in_mask(MASKS[n], place(dz, dy)))
                    def _(n=n):
                        part = rows_of(n)
                        remote(land.at[n, part], land.at[n, part], ssem.at[n], rsem.at[n], me).wait_recv()
                        acc[s, part] += land[n, part].astype(jnp.float32)

            if s == OWN:
                continue
            out[s] = acc[s].astype(jnp.bfloat16)
            for n, (t, parent, dz, dy) in enumerate(EDGES):
                if t == s and MASKS[n]:

                    @pl.when(in_mask(MASKS[n], me))
                    def _(n=n, dz=dz, dy=dy):
                        part = rows_of(n)
                        remote(out.at[s, part], land.at[n, part], ssem.at[n], rsem.at[n], place(-dz, dy)).start()

    for s in SLOTS:
        relay = SLOT_MASKS[s] & ~NEED_MASKS[s]
        if relay:

            @pl.when(in_mask(relay, me))
            def _(s=s):
                acck[s] = jnp.zeros((ROWS, HEAD), jnp.float32)
                accv[s] = jnp.zeros((ROWS, HEAD), jnp.float32)

    @pl.when(row == 0)
    def _():
        arrive(1, 2)

    stage_a(following(jnp.int32(-1)), 0)

    def returning(step, half):
        use = in_mask(pick(step, tuple(NEED_MASKS[s] for s in back)), me)

        @pl.when((step == 1) & (row == 1))
        def _():
            arrive(1, 2)

        @pl.when(use)
        def _():
            stage_a(following(step), 1 - half)
            stage_b(pick(step, back), half)

        for n in range(15):
            due = [(slot_id(*slot), r) for slot, at in SENDS.items() for r in (0, 1) if at[r] == n]
            due = [(s, SLOT_MASKS[s] & (0xFF << (RING * r))) for s, r in due]
            if due:

                @pl.when(step == n)
                def _(due=due):
                    for s, mask in due:
                        if mask:

                            @pl.when(in_mask(mask, me))
                            def _(s=s):
                                add_children(s)

        return jnp.where(use, 1 - half, half)

    half = lax.fori_loop(0, 15, returning, jnp.int32(0))
    stage_b(OWN, half)

    for h in range(HEADS):
        dq[:, h * HEAD : (h + 1) * HEAD] = (dqt[:, h * ROWS : (h + 1) * ROWS].T * SCALE).astype(jnp.bfloat16)
    store = pltpu.make_async_copy(dq, dq_any, here.at[0])
    store.start()
    add_children(OWN)
    dv[...] = accv[OWN].astype(jnp.bfloat16)
    dk[...] = (acck[OWN] * SCALE).astype(jnp.bfloat16)

    for n, (t, parent, dz, dy) in enumerate(EDGES):
        if MASKS[n]:

            @pl.when(in_mask(MASKS[n], place(dz, dy)))
            def _(n=n):
                part = rows_of(n)
                for buf, ssem, rsem in gathers:
                    remote(buf.at[0, part], buf.at[0, part], ssem.at[n], rsem.at[0], me).wait_send()

            @pl.when(in_mask(MASKS[n], me))
            def _(n=n):
                part = rows_of(n)
                for _, out, land, ssem, rsem in returns:
                    remote(out.at[0, part], land.at[n, part], ssem.at[n], rsem.at[n], me).wait_send()

    store.wait()


def hand_over(dq, dk, dv, dq_out, dk_out, dv_out):
    dq_out[...] = dq[...]
    dk_out[...] = dk[...]
    dv_out[...] = dv[...]


def local(queries, keys, values, attn_out, out_grad, tile_doc):
    vmem = pl.BlockSpec(memory_space=pltpu.VMEM)
    bf16, f32 = jnp.bfloat16, jnp.float32
    any_ = pl.BlockSpec(memory_space=pl.ANY)
    shapes = (
        jax.ShapeDtypeStruct((ROWS, HEADS * HEAD), bf16),
        jax.ShapeDtypeStruct((ROWS, HEAD), bf16),
        jax.ShapeDtypeStruct((ROWS, HEAD), bf16),
    )
    results = pl.pallas_call(
        kernel,
        out_shape=shapes,
        in_specs=[pl.BlockSpec(memory_space=pltpu.SMEM), any_, vmem, vmem, any_, any_],
        out_specs=(any_, vmem, vmem),
        scratch_shapes=[pltpu.VMEM((ROWS, HEADS * HEAD), bf16)] * 4
        + [
            pltpu.VMEM((2 * HEAD, WIDE), bf16),
            pltpu.VMEM((2 * HEAD, WIDE), bf16),
            pltpu.VMEM((WIDE, HEAD), bf16),
            pltpu.VMEM((WIDE, HEAD), bf16),
            pltpu.VMEM((16, ROWS, HEAD), bf16),
            pltpu.VMEM((16, ROWS, HEAD), bf16),
            pltpu.VMEM((16, HEADS, ROWS, ROWS), f32),
            pltpu.VMEM((16, 8, WIDE), f32),
            pltpu.VMEM((8, WIDE), f32),
            pltpu.VMEM((8, WIDE), f32),
            pltpu.VMEM((8, WIDE), f32),
            pltpu.VMEM((HEAD, WIDE), f32),
            pltpu.VMEM((2, ROWS, WIDE), bf16),
            pltpu.VMEM((2, ROWS, WIDE), bf16),
            pltpu.VMEM((16, ROWS, HEAD), f32),
            pltpu.VMEM((16, ROWS, HEAD), f32),
            pltpu.VMEM((16, ROWS, HEAD), bf16),
            pltpu.VMEM((16, ROWS, HEAD), bf16),
            pltpu.VMEM((len(EDGES), ROWS, HEAD), bf16),
            pltpu.VMEM((len(EDGES), ROWS, HEAD), bf16),
        ]
        + [pltpu.SemaphoreType.DMA((len(EDGES),))] * 8
        + [pltpu.SemaphoreType.DMA((3,))],
        compiler_params=pltpu.CompilerParams(
            collective_id=0, has_side_effects=True, vmem_limit_bytes=60 * 2**20
        ),
        name="attention_backward",
    )(tile_doc, queries, keys, values, attn_out, out_grad)
    return pl.pallas_call(
        hand_over,
        out_shape=shapes,
        in_specs=[vmem] * 3,
        out_specs=(vmem,) * 3,
        name="hand_over",
    )(*results)


def solution(mesh):
    rows = P(("seq", "ctx"), None)
    return jax.shard_map(
        local,
        mesh=mesh,
        in_specs=(rows, rows, rows, rows, rows, P("seq")),
        out_specs=(rows, rows, rows),
        check_vma=False,
    )
```

```python
import math

import jax
import jax.numpy as jnp
from jax import lax
from jax.experimental import pallas as pl
from jax.experimental.pallas import tpu as pltpu
from jax.sharding import PartitionSpec as P

HEADS = 8
HEAD = 128
ROWS = 256
WIDE = HEADS * ROWS
RING = 8
SCALE = 1.0 / math.sqrt(HEAD)
LOG2_SCALE = SCALE * math.log2(math.e)
BIG = float(2.0**100)
OWN = 3
REACH = 12

ORDER = (
    (0, -1), (1, 0), (0, 1), (0, -2), (0, 2),
    (1, -1), (1, 1), (1, -2), (1, 2), (0, -3), (0, 3),
    (1, -3), (1, 3), (0, 4), (1, 4),
)
BACK = (
    (1, -1), (1, -2), (1, 4), (0, 4), (1, -3), (0, -1), (1, 3), (0, -3), (0, 3), (1, 1),
    (1, 2), (0, 2), (0, -2), (0, 1), (1, 0),
)
SENDS = {
    (1, -1): (0, 0), (1, 4): (2, 2), (0, 4): (3, 3), (1, -3): (4, 4), (0, -1): (5, 5), (1, 3): (6, 6), (0, -3): (8, 8),
    (1, -2): (8, 8), (0, 3): (8, 8), (1, 1): (9, 9), (1, 2): (10, 10), (0, 2): (14, 12), (0, -2): (13, 12),
    (0, 1): (13, 13), (1, 0): (14, 14),
}
ARRIVALS = (
    ((0, -2), (0, 2), (0, -1), (0, 1), (1, 0)),
    ((1, -2), (1, 2), (0, -3), (0, 3), (1, -1), (1, 1)),
    ((1, -3), (1, 3), (0, 4), (1, 4)),
)
KEY_STEPS = (0, 3, 9)
VALUE_STEPS = (5,10)


def slot_id(r, d):
    return d + 3 if r == 0 else d + 11


SLOTS = tuple(slot_id(r, d) for r, d in ORDER)

RAW_EDGES = (
    ((0, -2), (0, 0), 2, 0, lambda r, z: True),
    ((0, 2), (0, 0), -2, 0, lambda r, z: True),
    ((0, -1), (0, 0), 1, 0, lambda r, z: True),
    ((0, 1), (0, 0), -1, 0, lambda r, z: True),
    ((1, 0), (0, 0), 0, 1, lambda r, z: r == 1),
    ((1, -2), (0, -2), 0, 1, lambda r, z: r == 1),
    ((1, 2), (0, 2), 0, 1, lambda r, z: r == 1),
    ((1, -1), (0, -1), 0, 1, lambda r, z: r == 1),
    ((1, 1), (1, 0), -1, 0, lambda r, z: r == 1),
    ((0, -3), (0, -2), 1, 0, lambda r, z: True),
    ((0, 3), (0, 2), -1, 0, lambda r, z: True),
    ((1, -3), (0, -3), 0, 1, lambda r, z: r == 1 and z >= 3),
    ((1, -3), (1, -2), 1, 0, lambda r, z: r == 1 and z < 3),
    ((1, 3), (1, 2), -1, 0, lambda r, z: r == 1),
    ((0, 4), (0, -3), 1, 0, lambda r, z: True),
    ((1, 4), (1, -2), 2, 0, lambda r, z: r == 1 and z >= 4),
    ((1, 4), (1, 2), -2, 0, lambda r, z: r == 1 and z < 4),
)
HALF_EDGE = 15


def plan():
    masks = [0] * len(RAW_EDGES)
    todo = []
    for me in range(2 * RING):
        row, z = divmod(me, RING)
        for r, d in ORDER:
            block = (row if r == 0 else 1 - row) * RING + (z + d) % RING
            if me - REACH <= block < me:
                todo.append((row, z, (r, d)))
    while todo:
        row, z, slot = todo.pop()
        if slot == (0, 0):
            continue
        found = [n for n, edge in enumerate(RAW_EDGES) if edge[0] == slot and edge[4](row, z)]
        assert len(found) == 1, (row, z, slot)
        bit = 1 << (row * RING + z)
        if not masks[found[0]] & bit:
            masks[found[0]] |= bit
            _, parent, dz, dy, _ = RAW_EDGES[found[0]]
            todo.append((row ^ dy, (z - dz) % RING, parent))
    return masks


MASKS = plan()
NEEDED = tuple(
    sum(
        1 << me
        for me in range(2 * RING)
        if me - REACH <= (me // RING ^ r) * RING + (me % RING + d) % RING < me
    )
    for r, d in ORDER
)
EDGES = tuple((slot_id(*t), slot_id(*p), dz, dy) for t, p, dz, dy, _ in RAW_EDGES)
for child, parent, _, _, _ in RAW_EDGES:
    assert parent == (0, 0) or all(a < b for a in SENDS[child] for b in SENDS[parent])
TILE = ROWS // 2
FAR = slot_id(1, 4)
FAR_MASK = MASKS[HALF_EDGE]
NEEDED = tuple(m & ~FAR_MASK if s == FAR else m for s, m in zip(SLOTS, NEEDED))
NEED_MASKS = dict(zip(SLOTS, NEEDED))
SLOT_MASKS = {s: sum(m for m, e in zip(MASKS, EDGES) if e[0] == s) for s in range(16)}


def dot(a, b):
    return lax.dot_general(a, b, (((1,), (0,)), ((), ())), preferred_element_type=jnp.float32)


def pick(index, values):
    out = jnp.int32(values[0])
    for i in range(1, len(values)):
        out = jnp.where(index == i, jnp.int32(values[i]), out)
    return out


def kernel(
    docs, q_any, k, v, o_any, do_any, dq_any, dk, dv,
    q, o, do, dq, qt, dot_, qb, dob, kall, vall, ebuf, seen, top, total, lse, dqt, pbuf, dsbuf, acck, accv,
    sendk, sendv, landk, landv, pfar, dsfar, kgs, kgr, vgs, vgr, krs, krr, vrs, vrr, here,
):
    me = lax.axis_index("ctx")
    row = me // RING
    z = me % RING

    def place(dz, dy):
        other = 1 - row if dy else row
        return other * RING + (z + dz + RING) % RING

    def in_mask(mask, device):
        return (jnp.int32(mask) >> device) & 1 == 1

    near = [(1, 0), (-1, 0), (2, 0), (-2, 0), (0, 1)]
    barrier = pltpu.get_barrier_semaphore()
    for dz, dy in near:
        pl.semaphore_signal(barrier, inc=1, device_id={"ctx": place(dz, dy)}, device_id_type=pl.DeviceIdType.MESH)

    loads = [
        pltpu.make_async_copy(src, dst, here.at[n])
        for n, (src, dst) in enumerate(((q_any, q), (do_any, do), (o_any, o)))
    ]
    for load in loads:
        load.start()
    kall[OWN] = k[...]
    vall[OWN] = v[...]
    pl.semaphore_wait(barrier, len(near))

    def remote(src, dst, ssem, rsem, target):
        return pltpu.make_async_remote_copy(
            src_ref=src, dst_ref=dst, send_sem=ssem, recv_sem=rsem,
            device_id={"ctx": target}, device_id_type=pl.DeviceIdType.MESH,
        )

    def rows_of(n):
        return pl.ds(ROWS // 2, ROWS // 2) if n == HALF_EDGE else pl.ds(0, ROWS)

    gathers = ((kall, kgs, kgr), (vall, vgs, vgr))

    def forward(which, s):
        buf, ssem, rsem = gathers[which]
        for n, (t, parent, dz, dy) in enumerate(EDGES):
            if parent == s and MASKS[n]:
                target = place(dz, dy)

                @pl.when(in_mask(MASKS[n], target))
                def _(n=n, t=t, target=target):
                    part = rows_of(n)
                    remote(buf.at[s, part], buf.at[t, part], ssem.at[n], rsem.at[t], target).start()

    def arrive(which, stage):
        buf, _, rsem = gathers[which]
        for r, d in ARRIVALS[stage]:
            s = slot_id(r, d)
            for n, edge in enumerate(EDGES):
                if edge[0] == s and MASKS[n]:

                    @pl.when(in_mask(MASKS[n], me))
                    def _(n=n):
                        part = rows_of(n)
                        remote(buf.at[s, part], buf.at[s, part], here.at[0], rsem.at[s], me).wait_recv()

            if SLOT_MASKS[s]:

                @pl.when(in_mask(SLOT_MASKS[s], me))
                def _(s=s):
                    forward(which, s)

    forward(0, OWN)
    for load in loads:
        load.wait()

    row16 = lax.broadcasted_iota(jnp.int32, (16, ROWS), 0)
    lane = lax.broadcasted_iota(jnp.int32, (ROWS, HEAD), 1)
    rowk = lax.broadcasted_iota(jnp.int32, (ROWS, HEAD), 0)
    qdoc = jnp.where(lax.broadcasted_iota(jnp.int32, (16, ROWS), 1) < 128, docs[2 * me], docs[2 * me + 1])
    mask_rows = jnp.where((row16 < 8) & (row16 != qdoc), -BIG, 0.0).astype(jnp.bfloat16)
    zeros = jnp.zeros((112, ROWS), jnp.bfloat16)
    for h in range(HEADS):
        sl = slice(h * ROWS, (h + 1) * ROWS)
        cols = slice(h * HEAD, (h + 1) * HEAD)
        qh, dh = q[:, cols], do[:, cols]
        qb[sl, :] = qh
        dob[sl, :] = dh
        qt[:HEAD, sl] = qh.T
        qt[HEAD : HEAD + 16, sl] = mask_rows
        qt[HEAD + 16 :, sl] = zeros
        dot_[:HEAD, sl] = dh.T
        prod = dh.astype(jnp.float32) * o[:, cols].astype(jnp.float32)
        minus = -jnp.sum(prod.T, axis=0, keepdims=True)
        hi = minus.astype(jnp.bfloat16).astype(jnp.float32)
        mid = (minus - hi).astype(jnp.bfloat16).astype(jnp.float32)
        low = minus - hi - mid
        rows = jnp.where(row16 == 0, hi, jnp.where(row16 == 1, mid, jnp.where(row16 == 2, low, 0.0)))
        dot_[HEAD : HEAD + 16, sl] = rows.astype(jnp.bfloat16)
        dot_[HEAD + 16 :, sl] = zeros
    dqt[...] = jnp.zeros_like(dqt)

    def block_of(s):
        far = s >= 8
        d = jnp.where(far, s - 11, s - 3)
        brow = jnp.where(far, 1 - row, row)
        return brow * RING + (z + d + RING) % RING

    def first_pass(s, own):
        b = me if own else block_of(s)
        kdoc = jnp.where(rowk < 128, docs[2 * b], docs[2 * b + 1])
        hot = jnp.where(lane == kdoc, 1.0, 0.0).astype(jnp.bfloat16)
        ka = jnp.concatenate([kall[s], hot], axis=1)
        for h in range(HEADS):
            sl = slice(h * ROWS, (h + 1) * ROWS)
            score = dot(ka, qt[:, sl])
            if own:
                keep = lax.broadcasted_iota(jnp.int32, (ROWS, ROWS), 0) <= lax.broadcasted_iota(
                    jnp.int32, (ROWS, ROWS), 1
                )
                score = jnp.where(keep, score, -BIG)
            score = score.reshape(ROWS // 8, 8, ROWS)
            new = jnp.max(score, axis=0)
            if not own:
                old = top[:, sl]
                new = jnp.maximum(old, new)
            e = jnp.exp2((score - new[None]) * LOG2_SCALE)
            added = jnp.sum(e, axis=0)
            if not own:
                added = added + total[:, sl] * jnp.exp2((old - new) * LOG2_SCALE)
            total[:, sl] = added
            top[:, sl] = new
            seen[s, :, sl] = new
            ebuf[s, h] = e.reshape(ROWS, ROWS)

    def pairs():
        for h in range(0, HEADS, 2):
            yield h, slice(h * ROWS, h * ROWS + TILE), slice((h + 1) * ROWS, (h + 1) * ROWS + TILE)

    def first_pass_far():
        hot = jnp.where(lane[:TILE] == docs[2 * block_of(FAR) + 1], 1.0, 0.0).astype(jnp.bfloat16)
        ka = jnp.concatenate([kall[FAR, TILE:], hot], axis=1)
        for h, one, two in pairs():
            both = dot(ka, jnp.concatenate([qt[:, one], qt[:, two]], axis=1))
            for n, sl in enumerate((one, two)):
                score = both[:, n * TILE : (n + 1) * TILE].reshape(TILE // 8, 8, TILE)
                old = top[:, sl]
                new = jnp.maximum(old, jnp.max(score, axis=0))
                e = jnp.exp2((score - new[None]) * LOG2_SCALE)
                total[:, sl] = jnp.sum(e, axis=0) + total[:, sl] * jnp.exp2((old - new) * LOG2_SCALE)
                top[:, sl] = new
                seen[FAR, :, sl] = new
                ebuf[FAR, h + n, :TILE, :TILE] = e.reshape(TILE, TILE)

    first_pass(OWN, True)

    @pl.loop(0, 15)
    def _(step):
        for n in range(15):
            due = [(w, i) for w, steps in ((0, KEY_STEPS), (1, VALUE_STEPS)) for i, at in enumerate(steps) if at == n]
            if due:

                @pl.when(step == n)
                def _(due=due):
                    for which, stage in due:
                        arrive(which, stage)
                        if which == 0 and stage == 0:
                            forward(1, OWN)

        @pl.when(in_mask(pick(step, NEEDED), me))
        def _():
            first_pass(pick(step, SLOTS), False)

        @pl.when((step == SLOTS.index(FAR)) & in_mask(FAR_MASK, me))
        def _():
            first_pass_far()

    peak = jnp.max(top[...], axis=0, keepdims=True)
    norm = jnp.sum(total[...] * jnp.exp2((top[...] - peak) * LOG2_SCALE), axis=0, keepdims=True)
    top[...] = jnp.broadcast_to(peak, (8, WIDE))
    lse[...] = jnp.broadcast_to(jnp.log2(norm), (8, WIDE))

    ones = jnp.where(lane < 3, 1.0, 0.0).astype(jnp.bfloat16)

    def stage_a(s, half):
        va = jnp.concatenate([vall[s], ones], axis=1)
        for h in range(HEADS):
            sl = slice(h * ROWS, (h + 1) * ROWS)
            inner = dot(va, dot_[:, sl])
            factor = jnp.exp2((seen[s, :, sl] - top[:, sl]) * LOG2_SCALE - lse[:, sl])
            prob = (ebuf[s, h].reshape(ROWS // 8, 8, ROWS) * factor[None]).reshape(ROWS, ROWS)
            pbuf[half, :, sl] = prob.astype(jnp.bfloat16)
            dsbuf[half, :, sl] = (prob * inner).astype(jnp.bfloat16)

    def stage_b(s, half):
        accv[s] = dot(pbuf[half], dob[...])
        acck[s] = dot(dsbuf[half], qb[...])
        dqt[...] += dot(kall[s].T, dsbuf[half])

    def second_pass_far():
        va = jnp.concatenate([vall[FAR, TILE:], ones[:TILE]], axis=1)
        for h, one, two in pairs():
            both = dot(va, jnp.concatenate([dot_[:, one], dot_[:, two]], axis=1))
            for n, sl in enumerate((one, two)):
                factor = jnp.exp2((seen[FAR, :, sl] - top[:, sl]) * LOG2_SCALE - lse[:, sl])
                prob = ebuf[FAR, h + n, :TILE, :TILE].reshape(TILE // 8, 8, TILE) * factor[None]
                prob = prob.reshape(TILE, TILE)
                cols = slice((h + n) * TILE, (h + n + 1) * TILE)
                pfar[:, cols] = prob.astype(jnp.bfloat16)
                dsfar[:, cols] = (prob * both[:, n * TILE : (n + 1) * TILE]).astype(jnp.bfloat16)
        firsts = [slice(h * ROWS, h * ROWS + TILE) for h in range(HEADS)]
        accv[FAR, TILE:] = dot(pfar[...], jnp.concatenate([dob[sl, :] for sl in firsts], axis=0))
        acck[FAR, TILE:] = dot(dsfar[...], jnp.concatenate([qb[sl, :] for sl in firsts], axis=0))
        part = dot(kall[FAR, TILE:].T, dsfar[...])
        for h, sl in enumerate(firsts):
            dqt[:, sl] += part[:, h * TILE : (h + 1) * TILE]

    back = tuple(slot_id(r, d) for r, d in BACK)

    def following(step):
        out = jnp.int32(OWN)
        for i in reversed(range(15)):
            out = jnp.where((step < i) & in_mask(NEED_MASKS[back[i]], me), jnp.int32(back[i]), out)
        return out

    returns = ((accv, sendv, landv, vrs, vrr), (acck, sendk, landk, krs, krr))

    def add_children(s):
        for acc, out, land, ssem, rsem in returns:
            for n, (t, parent, dz, dy) in enumerate(EDGES):
                if parent == s and MASKS[n]:

                    @pl.when(in_mask(MASKS[n], place(dz, dy)))
                    def _(n=n):
                        part = rows_of(n)
                        remote(land.at[n, part], land.at[n, part], ssem.at[n], rsem.at[n], me).wait_recv()
                        acc[s, part] += land[n, part].astype(jnp.float32)

            if s == OWN:
                continue
            out[s] = acc[s].astype(jnp.bfloat16)
            for n, (t, parent, dz, dy) in enumerate(EDGES):
                if t == s and MASKS[n]:

                    @pl.when(in_mask(MASKS[n], me))
                    def _(n=n, dz=dz, dy=dy):
                        part = rows_of(n)
                        remote(out.at[s, part], land.at[n, part], ssem.at[n], rsem.at[n], place(-dz, dy)).start()

    for s in SLOTS:
        relay = SLOT_MASKS[s] & ~NEED_MASKS[s]
        if relay:

            @pl.when(in_mask(relay, me))
            def _(s=s):
                acck[s] = jnp.zeros((ROWS, HEAD), jnp.float32)
                accv[s] = jnp.zeros((ROWS, HEAD), jnp.float32)

    @pl.when(row == 0)
    def _():
        arrive(1, 2)

    stage_a(following(jnp.int32(-1)), 0)

    def returning(step, half):
        use = in_mask(pick(step, tuple(NEED_MASKS[s] for s in back)), me)

        @pl.when((step == 1) & (row == 1))
        def _():
            arrive(1, 2)

        @pl.when(use)
        def _():
            stage_a(following(step), 1 - half)
            stage_b(pick(step, back), half)

        @pl.when((step == back.index(FAR)) & in_mask(FAR_MASK, me))
        def _():
            second_pass_far()

        for n in range(15):
            due = [(slot_id(*slot), r) for slot, at in SENDS.items() for r in (0, 1) if at[r] == n]
            due = [(s, SLOT_MASKS[s] & (0xFF << (RING * r))) for s, r in due]
            if due:

                @pl.when(step == n)
                def _(due=due):
                    for s, mask in due:
                        if mask:

                            @pl.when(in_mask(mask, me))
                            def _(s=s):
                                add_children(s)

        return jnp.where(use, 1 - half, half)

    half = lax.fori_loop(0, 15, returning, jnp.int32(0))
    stage_b(OWN, half)

    for h in range(HEADS):
        dq[:, h * HEAD : (h + 1) * HEAD] = (dqt[:, h * ROWS : (h + 1) * ROWS].T * SCALE).astype(jnp.bfloat16)
    store = pltpu.make_async_copy(dq, dq_any, here.at[0])
    store.start()
    add_children(OWN)
    dv[...] = accv[OWN].astype(jnp.bfloat16)
    dk[...] = (acck[OWN] * SCALE).astype(jnp.bfloat16)

    for n, (t, parent, dz, dy) in enumerate(EDGES):
        if MASKS[n]:

            @pl.when(in_mask(MASKS[n], place(dz, dy)))
            def _(n=n):
                part = rows_of(n)
                for buf, ssem, rsem in gathers:
                    remote(buf.at[0, part], buf.at[0, part], ssem.at[n], rsem.at[0], me).wait_send()

            @pl.when(in_mask(MASKS[n], me))
            def _(n=n):
                part = rows_of(n)
                for _, out, land, ssem, rsem in returns:
                    remote(out.at[0, part], land.at[n, part], ssem.at[n], rsem.at[n], me).wait_send()

    store.wait()


def hand_over(dq, dk, dv, dq_out, dk_out, dv_out):
    dq_out[...] = dq[...]
    dk_out[...] = dk[...]
    dv_out[...] = dv[...]


def local(queries, keys, values, attn_out, out_grad, tile_doc):
    vmem = pl.BlockSpec(memory_space=pltpu.VMEM)
    bf16, f32 = jnp.bfloat16, jnp.float32
    any_ = pl.BlockSpec(memory_space=pl.ANY)
    shapes = (
        jax.ShapeDtypeStruct((ROWS, HEADS * HEAD), bf16),
        jax.ShapeDtypeStruct((ROWS, HEAD), bf16),
        jax.ShapeDtypeStruct((ROWS, HEAD), bf16),
    )
    results = pl.pallas_call(
        kernel,
        out_shape=shapes,
        in_specs=[pl.BlockSpec(memory_space=pltpu.SMEM), any_, vmem, vmem, any_, any_],
        out_specs=(any_, vmem, vmem),
        scratch_shapes=[pltpu.VMEM((ROWS, HEADS * HEAD), bf16)] * 4
        + [
            pltpu.VMEM((2 * HEAD, WIDE), bf16),
            pltpu.VMEM((2 * HEAD, WIDE), bf16),
            pltpu.VMEM((WIDE, HEAD), bf16),
            pltpu.VMEM((WIDE, HEAD), bf16),
            pltpu.VMEM((16, ROWS, HEAD), bf16),
            pltpu.VMEM((16, ROWS, HEAD), bf16),
            pltpu.VMEM((16, HEADS, ROWS, ROWS), f32),
            pltpu.VMEM((16, 8, WIDE), f32),
            pltpu.VMEM((8, WIDE), f32),
            pltpu.VMEM((8, WIDE), f32),
            pltpu.VMEM((8, WIDE), f32),
            pltpu.VMEM((HEAD, WIDE), f32),
            pltpu.VMEM((2, ROWS, WIDE), bf16),
            pltpu.VMEM((2, ROWS, WIDE), bf16),
            pltpu.VMEM((16, ROWS, HEAD), f32),
            pltpu.VMEM((16, ROWS, HEAD), f32),
            pltpu.VMEM((16, ROWS, HEAD), bf16),
            pltpu.VMEM((16, ROWS, HEAD), bf16),
            pltpu.VMEM((len(EDGES), ROWS, HEAD), bf16),
            pltpu.VMEM((len(EDGES), ROWS, HEAD), bf16),
            pltpu.VMEM((TILE, HEADS * TILE), bf16),
            pltpu.VMEM((TILE, HEADS * TILE), bf16),
        ]
        + [pltpu.SemaphoreType.DMA((len(EDGES),))] * 8
        + [pltpu.SemaphoreType.DMA((3,))],
        compiler_params=pltpu.CompilerParams(
            collective_id=0, has_side_effects=True, vmem_limit_bytes=60 * 2**20
        ),
        name="attention_backward",
    )(tile_doc, queries, keys, values, attn_out, out_grad)
    return pl.pallas_call(
        hand_over,
        out_shape=shapes,
        in_specs=[vmem] * 3,
        out_specs=(vmem,) * 3,
        name="hand_over",
    )(*results)


def solution(mesh):
    rows = P(("seq", "ctx"), None)
    return jax.shard_map(
        local,
        mesh=mesh,
        in_specs=(rows, rows, rows, rows, rows, P("seq")),
        out_specs=(rows, rows, rows),
        check_vma=False,
    )
```

```python
import math

import jax
import jax.numpy as jnp
from jax import lax
from jax.experimental import pallas as pl
from jax.experimental.pallas import tpu as pltpu
from jax.sharding import PartitionSpec as P

HEADS = 8
HEAD = 128
ROWS = 256
WIDE = HEADS * ROWS
RING = 8
SCALE = 1.0 / math.sqrt(HEAD)
LOG2_SCALE = SCALE * math.log2(math.e)
BIG = float(2.0**100)
OWN = 3
REACH = 12

ORDER = (
    (0, -1), (1, 0), (0, 1), (0, -2), (0, 2),
    (1, -1), (1, 1), (1, -2), (1, 2), (0, -3), (0, 3),
    (1, -3), (1, 3), (0, 4), (1, 4),
)
BACK = (
    (1, -1), (1, -2), (1, 4), (0, 4), (1, -3), (0, -1), (1, 3), (0, -3), (0, 3), (1, 1),
    (1, 2), (0, 2), (0, -2), (0, 1), (1, 0),
)
SENDS = {
    (1, -1): (0, 0), (1, 4): (2, 2), (0, 4): (3, 3), (1, -3): (4, 4), (0, -1): (5, 5), (1, 3): (6, 6), (0, -3): (8, 8),
    (1, -2): (8, 8), (0, 3): (8, 8), (1, 1): (9, 9), (1, 2): (10, 10), (0, 2): (14, 12), (0, -2): (13, 12),
    (0, 1): (13, 13), (1, 0): (14, 14),
}
ARRIVALS = (
    ((0, -2), (0, 2), (0, -1), (0, 1), (1, 0)),
    ((1, -2), (1, 2), (0, -3), (0, 3), (1, -1), (1, 1)),
    ((1, -3), (1, 3), (0, 4), (1, 4)),
)
KEY_STEPS = (0, 3, 9)
VALUE_STEPS = (5,10)


def slot_id(r, d):
    return d + 3 if r == 0 else d + 11


SLOTS = tuple(slot_id(r, d) for r, d in ORDER)

RAW_EDGES = (
    ((0, -2), (0, 0), 2, 0, lambda r, z: True),
    ((0, 2), (0, 0), -2, 0, lambda r, z: True),
    ((0, -1), (0, 0), 1, 0, lambda r, z: True),
    ((0, 1), (0, 0), -1, 0, lambda r, z: True),
    ((1, 0), (0, 0), 0, 1, lambda r, z: r == 1),
    ((1, -2), (0, -2), 0, 1, lambda r, z: r == 1),
    ((1, 2), (0, 2), 0, 1, lambda r, z: r == 1),
    ((1, -1), (0, -1), 0, 1, lambda r, z: r == 1),
    ((1, 1), (1, 0), -1, 0, lambda r, z: r == 1),
    ((0, -3), (0, -2), 1, 0, lambda r, z: True),
    ((0, 3), (0, 2), -1, 0, lambda r, z: True),
    ((1, -3), (0, -3), 0, 1, lambda r, z: r == 1 and z >= 3),
    ((1, -3), (1, -2), 1, 0, lambda r, z: r == 1 and z < 3),
    ((1, 3), (1, 2), -1, 0, lambda r, z: r == 1),
    ((0, 4), (0, -3), 1, 0, lambda r, z: True),
    ((1, 4), (1, -2), 2, 0, lambda r, z: r == 1 and z >= 4),
    ((1, 4), (1, 2), -2, 0, lambda r, z: r == 1 and z < 4),
)
HALF_EDGE = 15


def plan():
    masks = [0] * len(RAW_EDGES)
    todo = []
    for me in range(2 * RING):
        row, z = divmod(me, RING)
        for r, d in ORDER:
            block = (row if r == 0 else 1 - row) * RING + (z + d) % RING
            if me - REACH <= block < me:
                todo.append((row, z, (r, d)))
    while todo:
        row, z, slot = todo.pop()
        if slot == (0, 0):
            continue
        found = [n for n, edge in enumerate(RAW_EDGES) if edge[0] == slot and edge[4](row, z)]
        assert len(found) == 1, (row, z, slot)
        bit = 1 << (row * RING + z)
        if not masks[found[0]] & bit:
            masks[found[0]] |= bit
            _, parent, dz, dy, _ = RAW_EDGES[found[0]]
            todo.append((row ^ dy, (z - dz) % RING, parent))
    return masks


MASKS = plan()
NEEDED = tuple(
    sum(
        1 << me
        for me in range(2 * RING)
        if me - REACH <= (me // RING ^ r) * RING + (me % RING + d) % RING < me
    )
    for r, d in ORDER
)
EDGES = tuple((slot_id(*t), slot_id(*p), dz, dy) for t, p, dz, dy, _ in RAW_EDGES)
for child, parent, _, _, _ in RAW_EDGES:
    assert parent == (0, 0) or all(a < b for a in SENDS[child] for b in SENDS[parent])
TILE = ROWS // 2
FAR = slot_id(1, 4)
FAR_MASK = MASKS[HALF_EDGE]
NEEDED = tuple(m & ~FAR_MASK if s == FAR else m for s, m in zip(SLOTS, NEEDED))
NEED_MASKS = dict(zip(SLOTS, NEEDED))
SLOT_MASKS = {s: sum(m for m, e in zip(MASKS, EDGES) if e[0] == s) for s in range(16)}


def dot(a, b):
    return lax.dot_general(a, b, (((1,), (0,)), ((), ())), preferred_element_type=jnp.float32)


def pick(index, values):
    out = jnp.int32(values[0])
    for i in range(1, len(values)):
        out = jnp.where(index == i, jnp.int32(values[i]), out)
    return out


def kernel(
    docs_any, q_any, k_any, v_any, o_any, do_any, dq_any, dk, dv,
    docs, q, o, do, dq, qt, dot_, qb, dob, kall, vall, ebuf, seen, top, total, lse, dqt, pbuf, dsbuf, acck, accv,
    sendk, sendv, landk, landv, pfar, dsfar, kgs, kgr, vgs, vgr, krs, krr, vrs, vrr, here,
):
    me = lax.axis_index("ctx")
    row = me // RING
    z = me % RING

    def place(dz, dy):
        other = 1 - row if dy else row
        return other * RING + (z + dz + RING) % RING

    def in_mask(mask, device):
        return (jnp.int32(mask) >> device) & 1 == 1

    near = [(1, 0), (-1, 0), (2, 0), (-2, 0), (0, 1)]
    barrier = pltpu.get_barrier_semaphore()
    for dz, dy in near:
        pl.semaphore_signal(barrier, inc=1, device_id={"ctx": place(dz, dy)}, device_id_type=pl.DeviceIdType.MESH)

    loads = [
        pltpu.make_async_copy(src, dst, here.at[n])
        for n, (src, dst) in enumerate(
            (
                (k_any, kall.at[OWN]), (v_any, vall.at[OWN]), (docs_any, docs),
                (q_any, q), (do_any, do), (o_any, o),
            )
        )
    ]
    for load in loads:
        load.start()
    pl.semaphore_wait(barrier, len(near))

    def remote(src, dst, ssem, rsem, target):
        return pltpu.make_async_remote_copy(
            src_ref=src, dst_ref=dst, send_sem=ssem, recv_sem=rsem,
            device_id={"ctx": target}, device_id_type=pl.DeviceIdType.MESH,
        )

    def rows_of(n):
        return pl.ds(ROWS // 2, ROWS // 2) if n == HALF_EDGE else pl.ds(0, ROWS)

    gathers = ((kall, kgs, kgr), (vall, vgs, vgr))

    def forward(which, s):
        buf, ssem, rsem = gathers[which]
        for n, (t, parent, dz, dy) in enumerate(EDGES):
            if parent == s and MASKS[n]:
                target = place(dz, dy)

                @pl.when(in_mask(MASKS[n], target))
                def _(n=n, t=t, target=target):
                    part = rows_of(n)
                    src = (k_any, v_any)[which] if s == OWN else buf.at[s, part]
                    remote(src, buf.at[t, part], ssem.at[n], rsem.at[t], target).start()

    def arrive(which, stage):
        buf, _, rsem = gathers[which]
        for r, d in ARRIVALS[stage]:
            s = slot_id(r, d)
            for n, edge in enumerate(EDGES):
                if edge[0] == s and MASKS[n]:

                    @pl.when(in_mask(MASKS[n], me))
                    def _(n=n):
                        part = rows_of(n)
                        remote(buf.at[s, part], buf.at[s, part], here.at[0], rsem.at[s], me).wait_recv()

            if SLOT_MASKS[s]:

                @pl.when(in_mask(SLOT_MASKS[s], me))
                def _(s=s):
                    forward(which, s)

    forward(0, OWN)
    for load in loads:
        load.wait()

    row16 = lax.broadcasted_iota(jnp.int32, (16, ROWS), 0)
    lane = lax.broadcasted_iota(jnp.int32, (ROWS, HEAD), 1)
    rowk = lax.broadcasted_iota(jnp.int32, (ROWS, HEAD), 0)
    qdoc = jnp.where(lax.broadcasted_iota(jnp.int32, (16, ROWS), 1) < 128, docs[2 * me], docs[2 * me + 1])
    mask_rows = jnp.where((row16 < 8) & (row16 != qdoc), -BIG, 0.0).astype(jnp.bfloat16)
    zeros = jnp.zeros((112, ROWS), jnp.bfloat16)
    for h in range(HEADS):
        sl = slice(h * ROWS, (h + 1) * ROWS)
        cols = slice(h * HEAD, (h + 1) * HEAD)
        qh, dh = q[:, cols], do[:, cols]
        qb[sl, :] = qh
        dob[sl, :] = dh
        qt[:HEAD, sl] = qh.T
        qt[HEAD : HEAD + 16, sl] = mask_rows
        qt[HEAD + 16 :, sl] = zeros
        dot_[:HEAD, sl] = dh.T
        prod = dh.astype(jnp.float32) * o[:, cols].astype(jnp.float32)
        minus = -jnp.sum(prod.T, axis=0, keepdims=True)
        hi = minus.astype(jnp.bfloat16).astype(jnp.float32)
        mid = (minus - hi).astype(jnp.bfloat16).astype(jnp.float32)
        low = minus - hi - mid
        rows = jnp.where(row16 == 0, hi, jnp.where(row16 == 1, mid, jnp.where(row16 == 2, low, 0.0)))
        dot_[HEAD : HEAD + 16, sl] = rows.astype(jnp.bfloat16)
        dot_[HEAD + 16 :, sl] = zeros
    dqt[...] = jnp.zeros_like(dqt)

    def block_of(s):
        far = s >= 8
        d = jnp.where(far, s - 11, s - 3)
        brow = jnp.where(far, 1 - row, row)
        return brow * RING + (z + d + RING) % RING

    def first_pass(s, own):
        b = me if own else block_of(s)
        kdoc = jnp.where(rowk < 128, docs[2 * b], docs[2 * b + 1])
        hot = jnp.where(lane == kdoc, 1.0, 0.0).astype(jnp.bfloat16)
        ka = jnp.concatenate([kall[s], hot], axis=1)
        for h in range(HEADS):
            sl = slice(h * ROWS, (h + 1) * ROWS)
            score = dot(ka, qt[:, sl])
            if own:
                keep = lax.broadcasted_iota(jnp.int32, (ROWS, ROWS), 0) <= lax.broadcasted_iota(
                    jnp.int32, (ROWS, ROWS), 1
                )
                score = jnp.where(keep, score, -BIG)
            score = score.reshape(ROWS // 8, 8, ROWS)
            new = jnp.max(score, axis=0)
            if not own:
                old = top[:, sl]
                new = jnp.maximum(old, new)
            e = jnp.exp2((score - new[None]) * LOG2_SCALE)
            added = jnp.sum(e, axis=0)
            if not own:
                added = added + total[:, sl] * jnp.exp2((old - new) * LOG2_SCALE)
            total[:, sl] = added
            top[:, sl] = new
            seen[s, :, sl] = new
            ebuf[s, h] = e.reshape(ROWS, ROWS)

    def pairs():
        for h in range(0, HEADS, 2):
            yield h, slice(h * ROWS, h * ROWS + TILE), slice((h + 1) * ROWS, (h + 1) * ROWS + TILE)

    def first_pass_far():
        hot = jnp.where(lane[:TILE] == docs[2 * block_of(FAR) + 1], 1.0, 0.0).astype(jnp.bfloat16)
        ka = jnp.concatenate([kall[FAR, TILE:], hot], axis=1)
        for h, one, two in pairs():
            both = dot(ka, jnp.concatenate([qt[:, one], qt[:, two]], axis=1))
            for n, sl in enumerate((one, two)):
                score = both[:, n * TILE : (n + 1) * TILE].reshape(TILE // 8, 8, TILE)
                old = top[:, sl]
                new = jnp.maximum(old, jnp.max(score, axis=0))
                e = jnp.exp2((score - new[None]) * LOG2_SCALE)
                total[:, sl] = jnp.sum(e, axis=0) + total[:, sl] * jnp.exp2((old - new) * LOG2_SCALE)
                top[:, sl] = new
                seen[FAR, :, sl] = new
                ebuf[FAR, h + n, :TILE, :TILE] = e.reshape(TILE, TILE)

    first_pass(OWN, True)

    @pl.loop(0, 15)
    def _(step):
        for n in range(15):
            due = [(w, i) for w, steps in ((0, KEY_STEPS), (1, VALUE_STEPS)) for i, at in enumerate(steps) if at == n]
            if due:

                @pl.when(step == n)
                def _(due=due):
                    for which, stage in due:
                        arrive(which, stage)
                        if which == 0 and stage == 0:
                            forward(1, OWN)

        @pl.when(in_mask(pick(step, NEEDED), me))
        def _():
            first_pass(pick(step, SLOTS), False)

        @pl.when((step == SLOTS.index(FAR)) & in_mask(FAR_MASK, me))
        def _():
            first_pass_far()

    peak = jnp.max(top[...], axis=0, keepdims=True)
    norm = jnp.sum(total[...] * jnp.exp2((top[...] - peak) * LOG2_SCALE), axis=0, keepdims=True)
    top[...] = jnp.broadcast_to(peak, (8, WIDE))
    lse[...] = jnp.broadcast_to(jnp.log2(norm), (8, WIDE))

    ones = jnp.where(lane < 3, 1.0, 0.0).astype(jnp.bfloat16)

    def stage_a(s, half):
        va = jnp.concatenate([vall[s], ones], axis=1)
        for h in range(HEADS):
            sl = slice(h * ROWS, (h + 1) * ROWS)
            inner = dot(va, dot_[:, sl])
            factor = jnp.exp2((seen[s, :, sl] - top[:, sl]) * LOG2_SCALE - lse[:, sl])
            prob = (ebuf[s, h].reshape(ROWS // 8, 8, ROWS) * factor[None]).reshape(ROWS, ROWS)
            pbuf[half, :, sl] = prob.astype(jnp.bfloat16)
            dsbuf[half, :, sl] = (prob * inner).astype(jnp.bfloat16)

    def stage_b(s, half):
        accv[s] = dot(pbuf[half], dob[...])
        acck[s] = dot(dsbuf[half], qb[...])
        dqt[...] += dot(kall[s].T, dsbuf[half])

    def second_pass_far():
        va = jnp.concatenate([vall[FAR, TILE:], ones[:TILE]], axis=1)
        for h, one, two in pairs():
            both = dot(va, jnp.concatenate([dot_[:, one], dot_[:, two]], axis=1))
            for n, sl in enumerate((one, two)):
                factor = jnp.exp2((seen[FAR, :, sl] - top[:, sl]) * LOG2_SCALE - lse[:, sl])
                prob = ebuf[FAR, h + n, :TILE, :TILE].reshape(TILE // 8, 8, TILE) * factor[None]
                prob = prob.reshape(TILE, TILE)
                cols = slice((h + n) * TILE, (h + n + 1) * TILE)
                pfar[:, cols] = prob.astype(jnp.bfloat16)
                dsfar[:, cols] = (prob * both[:, n * TILE : (n + 1) * TILE]).astype(jnp.bfloat16)
        firsts = [slice(h * ROWS, h * ROWS + TILE) for h in range(HEADS)]
        accv[FAR, TILE:] = dot(pfar[...], jnp.concatenate([dob[sl, :] for sl in firsts], axis=0))
        acck[FAR, TILE:] = dot(dsfar[...], jnp.concatenate([qb[sl, :] for sl in firsts], axis=0))
        part = dot(kall[FAR, TILE:].T, dsfar[...])
        for h, sl in enumerate(firsts):
            dqt[:, sl] += part[:, h * TILE : (h + 1) * TILE]

    back = tuple(slot_id(r, d) for r, d in BACK)

    def following(step):
        out = jnp.int32(OWN)
        for i in reversed(range(15)):
            out = jnp.where((step < i) & in_mask(NEED_MASKS[back[i]], me), jnp.int32(back[i]), out)
        return out

    returns = ((accv, sendv, landv, vrs, vrr), (acck, sendk, landk, krs, krr))

    def add_children(s):
        for acc, out, land, ssem, rsem in returns:
            for n, (t, parent, dz, dy) in enumerate(EDGES):
                if parent == s and MASKS[n]:

                    @pl.when(in_mask(MASKS[n], place(dz, dy)))
                    def _(n=n):
                        part = rows_of(n)
                        remote(land.at[n, part], land.at[n, part], ssem.at[n], rsem.at[n], me).wait_recv()
                        acc[s, part] += land[n, part].astype(jnp.float32)

            if s == OWN:
                continue
            out[s] = acc[s].astype(jnp.bfloat16)
            for n, (t, parent, dz, dy) in enumerate(EDGES):
                if t == s and MASKS[n]:

                    @pl.when(in_mask(MASKS[n], me))
                    def _(n=n, dz=dz, dy=dy):
                        part = rows_of(n)
                        remote(out.at[s, part], land.at[n, part], ssem.at[n], rsem.at[n], place(-dz, dy)).start()

    for s in SLOTS:
        relay = SLOT_MASKS[s] & ~NEED_MASKS[s]
        if relay:

            @pl.when(in_mask(relay, me))
            def _(s=s):
                acck[s] = jnp.zeros((ROWS, HEAD), jnp.float32)
                accv[s] = jnp.zeros((ROWS, HEAD), jnp.float32)

    @pl.when(row == 0)
    def _():
        arrive(1, 2)

    stage_a(following(jnp.int32(-1)), 0)

    def returning(step, half):
        use = in_mask(pick(step, tuple(NEED_MASKS[s] for s in back)), me)

        @pl.when((step == 1) & (row == 1))
        def _():
            arrive(1, 2)

        @pl.when(use)
        def _():
            stage_a(following(step), 1 - half)
            stage_b(pick(step, back), half)

        @pl.when((step == back.index(FAR)) & in_mask(FAR_MASK, me))
        def _():
            second_pass_far()

        for n in range(15):
            due = [(slot_id(*slot), r) for slot, at in SENDS.items() for r in (0, 1) if at[r] == n]
            due = [(s, SLOT_MASKS[s] & (0xFF << (RING * r))) for s, r in due]
            if due:

                @pl.when(step == n)
                def _(due=due):
                    for s, mask in due:
                        if mask:

                            @pl.when(in_mask(mask, me))
                            def _(s=s):
                                add_children(s)

        return jnp.where(use, 1 - half, half)

    half = lax.fori_loop(0, 15, returning, jnp.int32(0))
    stage_b(OWN, half)

    for h in range(HEADS):
        dq[:, h * HEAD : (h + 1) * HEAD] = (dqt[:, h * ROWS : (h + 1) * ROWS].T * SCALE).astype(jnp.bfloat16)
    store = pltpu.make_async_copy(dq, dq_any, here.at[0])
    store.start()
    add_children(OWN)
    dv[...] = accv[OWN].astype(jnp.bfloat16)
    dk[...] = (acck[OWN] * SCALE).astype(jnp.bfloat16)

    for n, (t, parent, dz, dy) in enumerate(EDGES):
        if MASKS[n]:

            @pl.when(in_mask(MASKS[n], place(dz, dy)))
            def _(n=n):
                part = rows_of(n)
                for buf, ssem, rsem in gathers:
                    remote(buf.at[0, part], buf.at[0, part], ssem.at[n], rsem.at[0], me).wait_send()

            @pl.when(in_mask(MASKS[n], me))
            def _(n=n):
                part = rows_of(n)
                for _, out, land, ssem, rsem in returns:
                    remote(out.at[0, part], land.at[n, part], ssem.at[n], rsem.at[n], me).wait_send()

    store.wait()


def hand_over(dq, dk, dv, dq_out, dk_out, dv_out):
    dq_out[...] = dq[...]
    dk_out[...] = dk[...]
    dv_out[...] = dv[...]


def local(queries, keys, values, attn_out, out_grad, tile_doc):
    vmem = pl.BlockSpec(memory_space=pltpu.VMEM)
    bf16, f32 = jnp.bfloat16, jnp.float32
    any_ = pl.BlockSpec(memory_space=pl.ANY)
    shapes = (
        jax.ShapeDtypeStruct((ROWS, HEADS * HEAD), bf16),
        jax.ShapeDtypeStruct((ROWS, HEAD), bf16),
        jax.ShapeDtypeStruct((ROWS, HEAD), bf16),
    )
    results = pl.pallas_call(
        kernel,
        out_shape=shapes,
        in_specs=[any_] * 6,
        out_specs=(any_, vmem, vmem),
        scratch_shapes=[pltpu.SMEM((2 * RING * 2,), jnp.int32)]
        + [pltpu.VMEM((ROWS, HEADS * HEAD), bf16)] * 4
        + [
            pltpu.VMEM((2 * HEAD, WIDE), bf16),
            pltpu.VMEM((2 * HEAD, WIDE), bf16),
            pltpu.VMEM((WIDE, HEAD), bf16),
            pltpu.VMEM((WIDE, HEAD), bf16),
            pltpu.VMEM((16, ROWS, HEAD), bf16),
            pltpu.VMEM((16, ROWS, HEAD), bf16),
            pltpu.VMEM((16, HEADS, ROWS, ROWS), f32),
            pltpu.VMEM((16, 8, WIDE), f32),
            pltpu.VMEM((8, WIDE), f32),
            pltpu.VMEM((8, WIDE), f32),
            pltpu.VMEM((8, WIDE), f32),
            pltpu.VMEM((HEAD, WIDE), f32),
            pltpu.VMEM((2, ROWS, WIDE), bf16),
            pltpu.VMEM((2, ROWS, WIDE), bf16),
            pltpu.VMEM((16, ROWS, HEAD), f32),
            pltpu.VMEM((16, ROWS, HEAD), f32),
            pltpu.VMEM((16, ROWS, HEAD), bf16),
            pltpu.VMEM((16, ROWS, HEAD), bf16),
            pltpu.VMEM((len(EDGES), ROWS, HEAD), bf16),
            pltpu.VMEM((len(EDGES), ROWS, HEAD), bf16),
            pltpu.VMEM((TILE, HEADS * TILE), bf16),
            pltpu.VMEM((TILE, HEADS * TILE), bf16),
        ]
        + [pltpu.SemaphoreType.DMA((len(EDGES),))] * 8
        + [pltpu.SemaphoreType.DMA((6,))],
        compiler_params=pltpu.CompilerParams(
            collective_id=0, has_side_effects=True, vmem_limit_bytes=60 * 2**20
        ),
        name="attention_backward",
    )(tile_doc, queries, keys, values, attn_out, out_grad)
    return pl.pallas_call(
        hand_over,
        out_shape=shapes,
        in_specs=[vmem] * 3,
        out_specs=(vmem,) * 3,
        name="hand_over",
    )(*results)


def solution(mesh):
    rows = P(("seq", "ctx"), None)
    return jax.shard_map(
        local,
        mesh=mesh,
        in_specs=(rows, rows, rows, rows, rows, P("seq")),
        out_specs=(rows, rows, rows),
        check_vma=False,
    )
```

```python
import math

import jax
import jax.numpy as jnp
from jax import lax
from jax.experimental import pallas as pl
from jax.experimental.pallas import tpu as pltpu
from jax.sharding import PartitionSpec as P

HEADS = 8
HEAD = 128
ROWS = 256
WIDE = HEADS * ROWS
RING = 8
SCALE = 1.0 / math.sqrt(HEAD)
LOG2_SCALE = SCALE * math.log2(math.e)
BIG = float(2.0**100)
OWN = 3
REACH = 12

ORDER = (
    (0, -1), (1, 0), (0, 1), (0, -2), (0, 2),
    (1, -1), (1, 1), (1, -2), (1, 2), (0, -3), (0, 3),
    (1, -3), (1, 3), (0, 4), (1, 4),
)
BACK = (
    (1, -1), (1, -2), (1, 4), (0, 4), (1, -3), (0, -1), (1, 3), (0, -3), (0, 3), (1, 1),
    (1, 2), (0, 2), (0, -2), (0, 1), (1, 0),
)
SENDS = {
    (1, -1): (0, 0), (1, 4): (2, 2), (0, 4): (3, 3), (1, -3): (4, 4), (0, -1): (5, 5), (1, 3): (6, 6), (0, -3): (8, 8),
    (1, -2): (8, 8), (0, 3): (8, 8), (1, 1): (9, 9), (1, 2): (10, 10), (0, 2): (14, 12), (0, -2): (13, 12),
    (0, 1): (13, 13), (1, 0): (14, 14),
}
ARRIVALS = (
    ((0, -2), (0, 2), (0, -1), (0, 1), (1, 0)),
    ((1, -2), (1, 2), (0, -3), (0, 3), (1, -1), (1, 1)),
    ((1, -3), (1, 3), (0, 4), (1, 4)),
)
KEY_STEPS = (0, 3, 9)
VALUE_STEPS = (5,10)


def slot_id(r, d):
    return d + 3 if r == 0 else d + 11


SLOTS = tuple(slot_id(r, d) for r, d in ORDER)

RAW_EDGES = (
    ((0, -2), (0, 0), 2, 0, lambda r, z: True),
    ((0, 2), (0, 0), -2, 0, lambda r, z: True),
    ((0, -1), (0, 0), 1, 0, lambda r, z: True),
    ((0, 1), (0, 0), -1, 0, lambda r, z: True),
    ((1, 0), (0, 0), 0, 1, lambda r, z: r == 1),
    ((1, -2), (0, -2), 0, 1, lambda r, z: r == 1),
    ((1, 2), (0, 2), 0, 1, lambda r, z: r == 1),
    ((1, -1), (0, -1), 0, 1, lambda r, z: r == 1),
    ((1, 1), (1, 0), -1, 0, lambda r, z: r == 1),
    ((0, -3), (0, -2), 1, 0, lambda r, z: True),
    ((0, 3), (0, 2), -1, 0, lambda r, z: True),
    ((1, -3), (0, -3), 0, 1, lambda r, z: r == 1 and z >= 3),
    ((1, -3), (1, -2), 1, 0, lambda r, z: r == 1 and z < 3),
    ((1, 3), (1, 2), -1, 0, lambda r, z: r == 1),
    ((0, 4), (0, -3), 1, 0, lambda r, z: True),
    ((1, 4), (1, -2), 2, 0, lambda r, z: r == 1 and z >= 4),
    ((1, 4), (1, 2), -2, 0, lambda r, z: r == 1 and z < 4),
)
HALF_EDGE = 15


def plan():
    masks = [0] * len(RAW_EDGES)
    todo = []
    for me in range(2 * RING):
        row, z = divmod(me, RING)
        for r, d in ORDER:
            block = (row if r == 0 else 1 - row) * RING + (z + d) % RING
            if me - REACH <= block < me:
                todo.append((row, z, (r, d)))
    while todo:
        row, z, slot = todo.pop()
        if slot == (0, 0):
            continue
        found = [n for n, edge in enumerate(RAW_EDGES) if edge[0] == slot and edge[4](row, z)]
        assert len(found) == 1, (row, z, slot)
        bit = 1 << (row * RING + z)
        if not masks[found[0]] & bit:
            masks[found[0]] |= bit
            _, parent, dz, dy, _ = RAW_EDGES[found[0]]
            todo.append((row ^ dy, (z - dz) % RING, parent))
    return masks


MASKS = plan()
NEEDED = tuple(
    sum(
        1 << me
        for me in range(2 * RING)
        if me - REACH <= (me // RING ^ r) * RING + (me % RING + d) % RING < me
    )
    for r, d in ORDER
)
EDGES = tuple((slot_id(*t), slot_id(*p), dz, dy) for t, p, dz, dy, _ in RAW_EDGES)
for child, parent, _, _, _ in RAW_EDGES:
    assert parent == (0, 0) or all(a < b for a in SENDS[child] for b in SENDS[parent])
TILE = ROWS // 2
FAR = slot_id(1, 4)
FAR_MASK = MASKS[HALF_EDGE]
NEEDED = tuple(m & ~FAR_MASK if s == FAR else m for s, m in zip(SLOTS, NEEDED))
NEED_MASKS = dict(zip(SLOTS, NEEDED))
SLOT_MASKS = {s: sum(m for m, e in zip(MASKS, EDGES) if e[0] == s) for s in range(16)}


def dot(a, b):
    return lax.dot_general(a, b, (((1,), (0,)), ((), ())), preferred_element_type=jnp.float32)


def pick(index, values):
    out = jnp.int32(values[0])
    for i in range(1, len(values)):
        out = jnp.where(index == i, jnp.int32(values[i]), out)
    return out


def kernel(
    docs_any, q_any, k_any, v_any, o_any, do_any, dq_any, dk_any, dv_any,
    docs, q, o, do, dq, qt, dot_, qb, dob, kall, vall, ebuf, seen, top, total, lse, dqt, pbuf, dsbuf, acck, accv,
    sendk, sendv, landk, landv, pfar, dsfar, kgs, kgr, vgs, vgr, krs, krr, vrs, vrr, here,
):
    me = lax.axis_index("ctx")
    row = me // RING
    z = me % RING

    def place(dz, dy):
        other = 1 - row if dy else row
        return other * RING + (z + dz + RING) % RING

    def in_mask(mask, device):
        return (jnp.int32(mask) >> device) & 1 == 1

    near = [(1, 0), (-1, 0), (2, 0), (-2, 0), (0, 1)]
    barrier = pltpu.get_barrier_semaphore()
    for dz, dy in near:
        pl.semaphore_signal(barrier, inc=1, device_id={"ctx": place(dz, dy)}, device_id_type=pl.DeviceIdType.MESH)

    loads = [
        pltpu.make_async_copy(src, dst, here.at[n])
        for n, (src, dst) in enumerate(
            (
                (k_any, kall.at[OWN]), (v_any, vall.at[OWN]), (docs_any, docs),
                (q_any, q), (do_any, do), (o_any, o),
            )
        )
    ]
    for load in loads:
        load.start()
    pl.semaphore_wait(barrier, len(near))

    def remote(src, dst, ssem, rsem, target):
        return pltpu.make_async_remote_copy(
            src_ref=src, dst_ref=dst, send_sem=ssem, recv_sem=rsem,
            device_id={"ctx": target}, device_id_type=pl.DeviceIdType.MESH,
        )

    def rows_of(n):
        return pl.ds(ROWS // 2, ROWS // 2) if n == HALF_EDGE else pl.ds(0, ROWS)

    gathers = ((kall, kgs, kgr), (vall, vgs, vgr))

    def forward(which, s):
        buf, ssem, rsem = gathers[which]
        for n, (t, parent, dz, dy) in enumerate(EDGES):
            if parent == s and MASKS[n]:
                target = place(dz, dy)

                @pl.when(in_mask(MASKS[n], target))
                def _(n=n, t=t, target=target):
                    part = rows_of(n)
                    src = (k_any, v_any)[which] if s == OWN else buf.at[s, part]
                    remote(src, buf.at[t, part], ssem.at[n], rsem.at[t], target).start()

    def arrive(which, stage):
        buf, _, rsem = gathers[which]
        for r, d in ARRIVALS[stage]:
            s = slot_id(r, d)
            for n, edge in enumerate(EDGES):
                if edge[0] == s and MASKS[n]:

                    @pl.when(in_mask(MASKS[n], me))
                    def _(n=n):
                        part = rows_of(n)
                        remote(buf.at[s, part], buf.at[s, part], here.at[0], rsem.at[s], me).wait_recv()

            if SLOT_MASKS[s]:

                @pl.when(in_mask(SLOT_MASKS[s], me))
                def _(s=s):
                    forward(which, s)

    forward(0, OWN)
    for load in loads:
        load.wait()

    row16 = lax.broadcasted_iota(jnp.int32, (16, ROWS), 0)
    lane = lax.broadcasted_iota(jnp.int32, (ROWS, HEAD), 1)
    rowk = lax.broadcasted_iota(jnp.int32, (ROWS, HEAD), 0)
    qdoc = jnp.where(lax.broadcasted_iota(jnp.int32, (16, ROWS), 1) < 128, docs[2 * me], docs[2 * me + 1])
    mask_rows = jnp.where((row16 < 8) & (row16 != qdoc), -BIG, 0.0).astype(jnp.bfloat16)
    zeros = jnp.zeros((112, ROWS), jnp.bfloat16)
    for h in range(HEADS):
        sl = slice(h * ROWS, (h + 1) * ROWS)
        cols = slice(h * HEAD, (h + 1) * HEAD)
        qh, dh = q[:, cols], do[:, cols]
        qb[sl, :] = qh
        dob[sl, :] = dh
        qt[:HEAD, sl] = qh.T
        qt[HEAD : HEAD + 16, sl] = mask_rows
        qt[HEAD + 16 :, sl] = zeros
        dot_[:HEAD, sl] = dh.T
        prod = dh.astype(jnp.float32) * o[:, cols].astype(jnp.float32)
        minus = -jnp.sum(prod.T, axis=0, keepdims=True)
        hi = minus.astype(jnp.bfloat16).astype(jnp.float32)
        mid = (minus - hi).astype(jnp.bfloat16).astype(jnp.float32)
        low = minus - hi - mid
        rows = jnp.where(row16 == 0, hi, jnp.where(row16 == 1, mid, jnp.where(row16 == 2, low, 0.0)))
        dot_[HEAD : HEAD + 16, sl] = rows.astype(jnp.bfloat16)
        dot_[HEAD + 16 :, sl] = zeros
    dqt[...] = jnp.zeros_like(dqt)

    def block_of(s):
        far = s >= 8
        d = jnp.where(far, s - 11, s - 3)
        brow = jnp.where(far, 1 - row, row)
        return brow * RING + (z + d + RING) % RING

    def first_pass(s, own):
        b = me if own else block_of(s)
        kdoc = jnp.where(rowk < 128, docs[2 * b], docs[2 * b + 1])
        hot = jnp.where(lane == kdoc, 1.0, 0.0).astype(jnp.bfloat16)
        ka = jnp.concatenate([kall[s], hot], axis=1)
        for h in range(HEADS):
            sl = slice(h * ROWS, (h + 1) * ROWS)
            score = dot(ka, qt[:, sl])
            if own:
                keep = lax.broadcasted_iota(jnp.int32, (ROWS, ROWS), 0) <= lax.broadcasted_iota(
                    jnp.int32, (ROWS, ROWS), 1
                )
                score = jnp.where(keep, score, -BIG)
            score = score.reshape(ROWS // 8, 8, ROWS)
            new = jnp.max(score, axis=0)
            if not own:
                old = top[:, sl]
                new = jnp.maximum(old, new)
            e = jnp.exp2((score - new[None]) * LOG2_SCALE)
            added = jnp.sum(e, axis=0)
            if not own:
                added = added + total[:, sl] * jnp.exp2((old - new) * LOG2_SCALE)
            total[:, sl] = added
            top[:, sl] = new
            seen[s, :, sl] = new
            ebuf[s, h] = e.reshape(ROWS, ROWS)

    def pairs():
        for h in range(0, HEADS, 2):
            yield h, slice(h * ROWS, h * ROWS + TILE), slice((h + 1) * ROWS, (h + 1) * ROWS + TILE)

    def first_pass_far():
        hot = jnp.where(lane[:TILE] == docs[2 * block_of(FAR) + 1], 1.0, 0.0).astype(jnp.bfloat16)
        ka = jnp.concatenate([kall[FAR, TILE:], hot], axis=1)
        for h, one, two in pairs():
            both = dot(ka, jnp.concatenate([qt[:, one], qt[:, two]], axis=1))
            for n, sl in enumerate((one, two)):
                score = both[:, n * TILE : (n + 1) * TILE].reshape(TILE // 8, 8, TILE)
                old = top[:, sl]
                new = jnp.maximum(old, jnp.max(score, axis=0))
                e = jnp.exp2((score - new[None]) * LOG2_SCALE)
                total[:, sl] = jnp.sum(e, axis=0) + total[:, sl] * jnp.exp2((old - new) * LOG2_SCALE)
                top[:, sl] = new
                seen[FAR, :, sl] = new
                ebuf[FAR, h + n, :TILE, :TILE] = e.reshape(TILE, TILE)

    first_pass(OWN, True)

    @pl.loop(0, 15)
    def _(step):
        for n in range(15):
            due = [(w, i) for w, steps in ((0, KEY_STEPS), (1, VALUE_STEPS)) for i, at in enumerate(steps) if at == n]
            if due:

                @pl.when(step == n)
                def _(due=due):
                    for which, stage in due:
                        arrive(which, stage)
                        if which == 0 and stage == 0:
                            forward(1, OWN)

        @pl.when(in_mask(pick(step, NEEDED), me))
        def _():
            first_pass(pick(step, SLOTS), False)

        @pl.when((step == SLOTS.index(FAR)) & in_mask(FAR_MASK, me))
        def _():
            first_pass_far()

    peak = jnp.max(top[...], axis=0, keepdims=True)
    norm = jnp.sum(total[...] * jnp.exp2((top[...] - peak) * LOG2_SCALE), axis=0, keepdims=True)
    top[...] = jnp.broadcast_to(peak, (8, WIDE))
    lse[...] = jnp.broadcast_to(jnp.log2(norm), (8, WIDE))

    ones = jnp.where(lane < 3, 1.0, 0.0).astype(jnp.bfloat16)

    def stage_a(s, half):
        va = jnp.concatenate([vall[s], ones], axis=1)
        for h in range(HEADS):
            sl = slice(h * ROWS, (h + 1) * ROWS)
            inner = dot(va, dot_[:, sl])
            factor = jnp.exp2((seen[s, :, sl] - top[:, sl]) * LOG2_SCALE - lse[:, sl])
            prob = (ebuf[s, h].reshape(ROWS // 8, 8, ROWS) * factor[None]).reshape(ROWS, ROWS)
            pbuf[half, :, sl] = prob.astype(jnp.bfloat16)
            dsbuf[half, :, sl] = (prob * inner).astype(jnp.bfloat16)

    def stage_b(s, half):
        accv[s] = dot(pbuf[half], dob[...])
        acck[s] = dot(dsbuf[half], qb[...])
        dqt[...] += dot(kall[s].T, dsbuf[half])

    def second_pass_far():
        va = jnp.concatenate([vall[FAR, TILE:], ones[:TILE]], axis=1)
        for h, one, two in pairs():
            both = dot(va, jnp.concatenate([dot_[:, one], dot_[:, two]], axis=1))
            for n, sl in enumerate((one, two)):
                factor = jnp.exp2((seen[FAR, :, sl] - top[:, sl]) * LOG2_SCALE - lse[:, sl])
                prob = ebuf[FAR, h + n, :TILE, :TILE].reshape(TILE // 8, 8, TILE) * factor[None]
                prob = prob.reshape(TILE, TILE)
                cols = slice((h + n) * TILE, (h + n + 1) * TILE)
                pfar[:, cols] = prob.astype(jnp.bfloat16)
                dsfar[:, cols] = (prob * both[:, n * TILE : (n + 1) * TILE]).astype(jnp.bfloat16)
        firsts = [slice(h * ROWS, h * ROWS + TILE) for h in range(HEADS)]
        accv[FAR, TILE:] = dot(pfar[...], jnp.concatenate([dob[sl, :] for sl in firsts], axis=0))
        acck[FAR, TILE:] = dot(dsfar[...], jnp.concatenate([qb[sl, :] for sl in firsts], axis=0))
        part = dot(kall[FAR, TILE:].T, dsfar[...])
        for h, sl in enumerate(firsts):
            dqt[:, sl] += part[:, h * TILE : (h + 1) * TILE]

    back = tuple(slot_id(r, d) for r, d in BACK)

    def following(step):
        out = jnp.int32(OWN)
        for i in reversed(range(15)):
            out = jnp.where((step < i) & in_mask(NEED_MASKS[back[i]], me), jnp.int32(back[i]), out)
        return out

    returns = ((accv, sendv, landv, vrs, vrr), (acck, sendk, landk, krs, krr))

    def add_children(s):
        for acc, out, land, ssem, rsem in returns:
            for n, (t, parent, dz, dy) in enumerate(EDGES):
                if parent == s and MASKS[n]:

                    @pl.when(in_mask(MASKS[n], place(dz, dy)))
                    def _(n=n):
                        part = rows_of(n)
                        remote(land.at[n, part], land.at[n, part], ssem.at[n], rsem.at[n], me).wait_recv()
                        acc[s, part] += land[n, part].astype(jnp.float32)

            if s == OWN:
                continue
            out[s] = acc[s].astype(jnp.bfloat16)
            for n, (t, parent, dz, dy) in enumerate(EDGES):
                if t == s and MASKS[n]:

                    @pl.when(in_mask(MASKS[n], me))
                    def _(n=n, dz=dz, dy=dy):
                        part = rows_of(n)
                        remote(out.at[s, part], land.at[n, part], ssem.at[n], rsem.at[n], place(-dz, dy)).start()

    for s in SLOTS:
        relay = SLOT_MASKS[s] & ~NEED_MASKS[s]
        if relay:

            @pl.when(in_mask(relay, me))
            def _(s=s):
                acck[s] = jnp.zeros((ROWS, HEAD), jnp.float32)
                accv[s] = jnp.zeros((ROWS, HEAD), jnp.float32)

    @pl.when(row == 0)
    def _():
        arrive(1, 2)

    stage_a(following(jnp.int32(-1)), 0)

    def returning(step, half):
        use = in_mask(pick(step, tuple(NEED_MASKS[s] for s in back)), me)

        @pl.when((step == 1) & (row == 1))
        def _():
            arrive(1, 2)

        @pl.when(use)
        def _():
            stage_a(following(step), 1 - half)
            stage_b(pick(step, back), half)

        @pl.when((step == back.index(FAR)) & in_mask(FAR_MASK, me))
        def _():
            second_pass_far()

        for n in range(15):
            due = [(slot_id(*slot), r) for slot, at in SENDS.items() for r in (0, 1) if at[r] == n]
            due = [(s, SLOT_MASKS[s] & (0xFF << (RING * r))) for s, r in due]
            if due:

                @pl.when(step == n)
                def _(due=due):
                    for s, mask in due:
                        if mask:

                            @pl.when(in_mask(mask, me))
                            def _(s=s):
                                add_children(s)

        return jnp.where(use, 1 - half, half)

    half = lax.fori_loop(0, 15, returning, jnp.int32(0))
    stage_b(OWN, half)

    for h in range(HEADS):
        dq[:, h * HEAD : (h + 1) * HEAD] = (dqt[:, h * ROWS : (h + 1) * ROWS].T * SCALE).astype(jnp.bfloat16)
    store = pltpu.make_async_copy(dq, dq_any, here.at[0])
    store.start()
    add_children(OWN)
    sendv[OWN] = accv[OWN].astype(jnp.bfloat16)
    sendk[OWN] = (acck[OWN] * SCALE).astype(jnp.bfloat16)
    stores = [
        store,
        pltpu.make_async_copy(sendv.at[OWN], dv_any, here.at[1]),
        pltpu.make_async_copy(sendk.at[OWN], dk_any, here.at[2]),
    ]
    for copy in stores[1:]:
        copy.start()

    for n, (t, parent, dz, dy) in enumerate(EDGES):
        if MASKS[n]:

            @pl.when(in_mask(MASKS[n], place(dz, dy)))
            def _(n=n):
                part = rows_of(n)
                for buf, ssem, rsem in gathers:
                    remote(buf.at[0, part], buf.at[0, part], ssem.at[n], rsem.at[0], me).wait_send()

            @pl.when(in_mask(MASKS[n], me))
            def _(n=n):
                part = rows_of(n)
                for _, out, land, ssem, rsem in returns:
                    remote(out.at[0, part], land.at[n, part], ssem.at[n], rsem.at[n], me).wait_send()

    for copy in stores:
        copy.wait()


def hand_over(dq, dk, dv, dq_out, dk_out, dv_out):
    dq_out[...] = dq[...]
    dk_out[...] = dk[...]
    dv_out[...] = dv[...]


def local(queries, keys, values, attn_out, out_grad, tile_doc):
    vmem = pl.BlockSpec(memory_space=pltpu.VMEM)
    bf16, f32 = jnp.bfloat16, jnp.float32
    any_ = pl.BlockSpec(memory_space=pl.ANY)
    shapes = (
        jax.ShapeDtypeStruct((ROWS, HEADS * HEAD), bf16),
        jax.ShapeDtypeStruct((ROWS, HEAD), bf16),
        jax.ShapeDtypeStruct((ROWS, HEAD), bf16),
    )
    results = pl.pallas_call(
        kernel,
        out_shape=shapes,
        in_specs=[any_] * 6,
        out_specs=(any_,) * 3,
        scratch_shapes=[pltpu.SMEM((2 * RING * 2,), jnp.int32)]
        + [pltpu.VMEM((ROWS, HEADS * HEAD), bf16)] * 4
        + [
            pltpu.VMEM((2 * HEAD, WIDE), bf16),
            pltpu.VMEM((2 * HEAD, WIDE), bf16),
            pltpu.VMEM((WIDE, HEAD), bf16),
            pltpu.VMEM((WIDE, HEAD), bf16),
            pltpu.VMEM((16, ROWS, HEAD), bf16),
            pltpu.VMEM((16, ROWS, HEAD), bf16),
            pltpu.VMEM((16, HEADS, ROWS, ROWS), f32),
            pltpu.VMEM((16, 8, WIDE), f32),
            pltpu.VMEM((8, WIDE), f32),
            pltpu.VMEM((8, WIDE), f32),
            pltpu.VMEM((8, WIDE), f32),
            pltpu.VMEM((HEAD, WIDE), f32),
            pltpu.VMEM((2, ROWS, WIDE), bf16),
            pltpu.VMEM((2, ROWS, WIDE), bf16),
            pltpu.VMEM((16, ROWS, HEAD), f32),
            pltpu.VMEM((16, ROWS, HEAD), f32),
            pltpu.VMEM((16, ROWS, HEAD), bf16),
            pltpu.VMEM((16, ROWS, HEAD), bf16),
            pltpu.VMEM((len(EDGES), ROWS, HEAD), bf16),
            pltpu.VMEM((len(EDGES), ROWS, HEAD), bf16),
            pltpu.VMEM((TILE, HEADS * TILE), bf16),
            pltpu.VMEM((TILE, HEADS * TILE), bf16),
        ]
        + [pltpu.SemaphoreType.DMA((len(EDGES),))] * 8
        + [pltpu.SemaphoreType.DMA((6,))],
        compiler_params=pltpu.CompilerParams(
            collective_id=0, has_side_effects=True, vmem_limit_bytes=60 * 2**20
        ),
        name="attention_backward",
    )(tile_doc, queries, keys, values, attn_out, out_grad)
    return pl.pallas_call(
        hand_over,
        out_shape=shapes,
        in_specs=[vmem] * 3,
        out_specs=(vmem,) * 3,
        name="hand_over",
    )(*results)


def solution(mesh):
    rows = P(("seq", "ctx"), None)
    return jax.shard_map(
        local,
        mesh=mesh,
        in_specs=(rows, rows, rows, rows, rows, P("seq")),
        out_specs=(rows, rows, rows),
        check_vma=False,
    )
```
